32 devices in a mesh: seg: 4 (over x, core), seq: 8 (over z, y).
Axes of the slice: x: 2, y: 2, z: 4, core: 2. Of those that a mesh axis runs over, the one named last changes fastest.
Arguments:
- queries: bfloat16 [4096, 4096], P(('seg', 'seq')), may hold values from -6 to 6
- keys: bfloat16 [4096, 4096], P(('seg', 'seq')), may hold values from -6 to 6
- values: bfloat16 [4096, 4096], P(('seg', 'seq')), may hold values from -6 to 6
- prior_keys: bfloat16 [1024, 4096], P('seq'), may hold values from -6 to 6
- prior_values: bfloat16 [1024, 4096], P('seq'), may hold values from -6 to 6
- conv_keys: bfloat16 [32, 512, 128], P('seq'), may hold values from -0.5 to 0.5
- conv_values: bfloat16 [32, 512, 128], P('seq'), may hold values from -0.5 to 0.5
- doc_starts: int32 [4], replicated, may hold values from 0 to 2047, as said below
Outputs:
- attended: bfloat16 [4096, 4096], P(('seg', 'seq'))
- compressed_keys: bfloat16 [1024, 4096], P('seg', 'seq')
- compressed_values: bfloat16 [1024, 4096], P('seg', 'seq')
- recon_loss: float32 [], replicated
- grad_conv_keys: float32 [32, 512, 128], P('seq')
- grad_conv_values: float32 [32, 512, 128], P('seq')
The draws below stay inside these ranges and needn't reach their ends.
Inputs may be any that keep to these rules, and one draw needn't show every extreme that they name: `doc_starts`: entry g is the offset within segment g at which a document starts; an entry of 1024 or more means segment g continues the document before it. Entry 0 is 2047, entries 1 and 2 are 1024 or more, entry 3 lies from 512 to 1023.
All inputs are finite; a program needn't handle non-finite values.
Results may differ from the reference program's by a relative error of at most 0.015.
Values may be sent and summed in bfloat16 or wider, within the bound.
No kernel may reach another device: no remote copies, remote signals or barrier semaphores. Data moves between devices by JAX's collectives and lax.ppermute only.
A program may use at most 64 MiB of HBM per device.

```python
import math
import jax
import jax.numpy as jnp
from jax import lax

H = 32
DH = 128
RATE = 4
SEG_LEN = 1024
COMP_ROWS = 256
TOKENS = 4096
N_SEG = 4


def paired_rows(key):
    seeds = jax.random.split(jax.random.fold_in(key, 101), 2)
    shape = (TOKENS, H * DH)
    base_query = jnp.clip(jax.random.normal(seeds[0], shape, jnp.float32), -6.0, 6.0)
    base_key = jnp.clip(jax.random.normal(seeds[1], shape, jnp.float32), -6.0, 6.0)
    return (base_query, base_key)


def draw_queries(key, part):
    return paired_rows(key)[0].astype(jnp.bfloat16)


def draw_keys(key, part):
    return paired_rows(key)[1].astype(jnp.bfloat16)


def conv_draw(key, salt):
    inner_key = jax.random.fold_in(key, salt)
    shape = (H, RATE * DH, DH)
    spread = 0.5 / math.sqrt(RATE * DH)
    noise = jnp.clip(jax.random.normal(inner_key, shape, jnp.float32), -6.0, 6.0) * spread
    diagonal = (jnp.arange(RATE * DH)[:, None] % DH == jnp.arange(DH)[None, :]).astype(jnp.float32)
    return (0.25 * diagonal[None, :, :] + noise).astype(jnp.bfloat16)


def draw_conv_keys(key, part):
    return conv_draw(key, 211)


def draw_conv_values(key, part):
    return conv_draw(key, 307)


def draw_doc_starts(key, part):
    seeds = jax.random.split(jax.random.fold_in(key, 401), 4)
    segment_count = TOKENS // SEG_LEN
    general = jax.random.randint(seeds[0], (segment_count,), 0, 2 * SEG_LEN)
    continuing = jax.random.randint(seeds[1], (segment_count,), SEG_LEN, 2 * SEG_LEN)
    middle = jax.random.randint(seeds[2], (segment_count,), SEG_LEN // 2, SEG_LEN)
    early = jax.random.randint(seeds[3], (segment_count,), 0, SEG_LEN // 4)
    place = jnp.arange(segment_count)
    result = jnp.where(place == segment_count - 3, early, general)
    result = jnp.where(place == segment_count - 1, middle, result)
    result = jnp.where((place < 2) | (place == segment_count - 2), continuing, result)
    result = jnp.where(place == 0, 2 * SEG_LEN - 1, result)
    return result.astype(jnp.int32)


def steps_of(own_key, dims, cuts, low, largest):
    factor_of = 1.0
    for position, blocks in cuts:
        draws = jax.random.uniform(jax.random.fold_in(jax.random.fold_in(own_key, 6), position), (blocks,), jnp.float32, low / len(cuts), largest / len(cuts))
        factor_of = factor_of * jnp.repeat(jnp.exp(draws), dims[position] // blocks).reshape((-1,) + (1,) * (len(dims) - 1 - position))
    return factor_of


def normal_values(rng, extent, scale, limit, cuts=(), kind=jnp.bfloat16):
    factor_of = steps_of(rng, extent, cuts, -0.22, 0.18) if cuts else 1.0
    values = jax.random.normal(rng, extent, jnp.float32) * scale * factor_of
    return jnp.minimum(jnp.maximum(values, -limit), limit).astype(kind)


def setup_inputs(seed: int = 0) -> dict:
    streams_of = jax.random.split(jax.random.key(seed), 9)
    queries = draw_queries(jax.random.fold_in(streams_of[8], 71), 0)
    keys = draw_keys(jax.random.fold_in(streams_of[8], 71), 0)
    values = normal_values(streams_of[2], (TOKENS, H * DH), 1.0, 6.0, ((0, 32),))
    prior_keys = normal_values(streams_of[3], (SEG_LEN, H * DH), 1.0, 6.0, ((0, 8),))
    prior_values = normal_values(streams_of[4], (SEG_LEN, H * DH), 1.0, 6.0, ((0, 8),))
    conv_keys = draw_conv_keys(jax.random.fold_in(streams_of[8], 71), 0)
    conv_values = draw_conv_values(jax.random.fold_in(streams_of[8], 71), 0)
    doc_starts = draw_doc_starts(jax.random.fold_in(streams_of[8], 71), 0)
    return dict(queries=queries, keys=keys, values=values, prior_keys=prior_keys, prior_values=prior_values, conv_keys=conv_keys, conv_values=conv_values, doc_starts=doc_starts)


def visible_mask(group_index, doc_starts, query_place, column):
    comp_part = column < COMP_ROWS
    fine_part = (column >= COMP_ROWS) & (column < COMP_ROWS + SEG_LEN)
    own_part = column >= COMP_ROWS + SEG_LEN
    key_place = jnp.where(comp_part, RATE * column, jnp.where(fine_part, column - COMP_ROWS, column - COMP_ROWS - SEG_LEN))
    start_now = doc_starts[group_index]
    start_prev = jnp.where(group_index >= 1, doc_starts[jnp.maximum(group_index - 1, 0)], SEG_LEN)
    start_back = jnp.where(group_index >= 2, doc_starts[jnp.maximum(group_index - 2, 0)], SEG_LEN)
    lead_prev = jnp.where(start_prev < SEG_LEN, start_prev, 0)
    lead_back = jnp.where(start_back < SEG_LEN, start_back, 0)
    comp_open = (group_index >= 1) & (start_prev >= SEG_LEN)
    before_doc = query_place < start_now
    seen_comp = comp_part & comp_open & before_doc & (key_place >= lead_back)
    seen_fine = fine_part & before_doc & (key_place >= lead_prev)
    seen_own = own_part & (key_place <= query_place) & ((key_place >= start_now) | before_doc)
    return seen_comp | seen_fine | seen_own

def reference(queries, keys, values, prior_keys, prior_values, conv_keys, conv_values, doc_starts):
    score_scale = 1.0 / math.sqrt(DH)

    def by_head(flat_array):
        return flat_array.reshape(-1, SEG_LEN, H, DH).transpose(0, 2, 1, 3)
    query_heads = by_head(queries)
    key_heads = by_head(keys)
    value_heads = by_head(values)
    fine_keys = jnp.concatenate((by_head(prior_keys), key_heads[:-1]), axis=0)
    fine_values = jnp.concatenate((by_head(prior_values), value_heads[:-1]), axis=0)

    def compress(source_rows, weight):
        windows = source_rows.reshape(N_SEG, H, COMP_ROWS, RATE * DH).astype(jnp.float32)
        return jnp.einsum('ghcw,hwd->ghcd', windows, weight.astype(jnp.float32)).astype(jnp.bfloat16)
    comp_keys = compress(fine_keys, conv_keys)
    comp_values = compress(fine_values, conv_values)
    blank_rows = jnp.zeros((1, H, COMP_ROWS, DH), jnp.bfloat16)
    memory_keys = jnp.concatenate((blank_rows, comp_keys[:-1]), axis=0)
    memory_values = jnp.concatenate((blank_rows, comp_values[:-1]), axis=0)
    column = jnp.arange(COMP_ROWS + 2 * SEG_LEN, dtype=jnp.int32)[None, :]
    query_place = jnp.arange(SEG_LEN, dtype=jnp.int32)[:, None]

    def main_item(flat_index):
        group_index = flat_index // H
        head_index = flat_index % H
        query_rows = query_heads[group_index, head_index]
        key_rows = jnp.concatenate((memory_keys[group_index, head_index], fine_keys[group_index, head_index], key_heads[group_index, head_index]), axis=0)
        value_rows = jnp.concatenate((memory_values[group_index, head_index], fine_values[group_index, head_index], value_heads[group_index, head_index]), axis=0)
        visible = visible_mask(group_index, doc_starts, query_place, column)
        scores = jnp.dot(query_rows, key_rows.T, preferred_element_type=jnp.float32) * score_scale
        row_top = lax.optimization_barrier(jnp.max(jnp.where(visible, scores, -jnp.inf), axis=1, keepdims=True))
        weights = jnp.exp(jnp.where(visible, scores - row_top, -jnp.inf))
        row_total = lax.optimization_barrier(jnp.sum(weights, axis=1, keepdims=True))
        mixed_rows = jnp.dot(weights.astype(jnp.bfloat16), value_rows, preferred_element_type=jnp.float32) / row_total
        return mixed_rows.astype(jnp.bfloat16)
    attended = lax.map(main_item, jnp.arange(N_SEG * H, dtype=jnp.int32))
    attended = attended.reshape(N_SEG, H, SEG_LEN, DH).transpose(0, 2, 1, 3).reshape(TOKENS, H * DH)

    def recon_item(flat_index):
        group_index = flat_index // H
        head_index = flat_index % H
        query_rows = query_heads[group_index, head_index]
        fine_k = fine_keys[group_index, head_index]
        fine_v = fine_values[group_index, head_index]
        comp_k = comp_keys[group_index, head_index]
        comp_v = comp_values[group_index, head_index]
        fine_scores = jnp.dot(query_rows, fine_k.T, preferred_element_type=jnp.float32) * score_scale
        fine_exp = jnp.exp(fine_scores - lax.optimization_barrier(jnp.max(fine_scores, axis=1, keepdims=True)))
        fine_total = lax.optimization_barrier(jnp.sum(fine_exp, axis=1, keepdims=True))
        recon_fine = jnp.dot(fine_exp.astype(jnp.bfloat16), fine_v, preferred_element_type=jnp.float32) / fine_total
        comp_scores = jnp.dot(query_rows, comp_k.T, preferred_element_type=jnp.float32) * score_scale
        comp_exp = jnp.exp(comp_scores - lax.optimization_barrier(jnp.max(comp_scores, axis=1, keepdims=True)))
        comp_total = lax.optimization_barrier(jnp.sum(comp_exp, axis=1, keepdims=True))
        comp_weights = comp_exp.astype(jnp.bfloat16)
        recon_comp = jnp.dot(comp_weights, comp_v, preferred_element_type=jnp.float32) / comp_total
        differ = recon_fine - recon_comp
        out_grad = (-2.0 * differ / comp_total).astype(jnp.bfloat16)
        value_grad = jnp.dot(comp_weights.T, out_grad, preferred_element_type=jnp.float32).astype(jnp.bfloat16)
        inner_grad = jnp.dot(out_grad, comp_v.T, preferred_element_type=jnp.float32)
        row_offset = lax.optimization_barrier(jnp.sum(out_grad.astype(jnp.float32) * recon_comp, axis=1, keepdims=True))
        score_grad = (comp_exp * (inner_grad - row_offset)).astype(jnp.bfloat16)
        key_grad = (jnp.dot(score_grad.T, query_rows, preferred_element_type=jnp.float32) * score_scale).astype(jnp.bfloat16)
        windows_k = fine_k.reshape(COMP_ROWS, RATE * DH)
        windows_v = fine_v.reshape(COMP_ROWS, RATE * DH)
        grad_k = jnp.dot(windows_k.T, key_grad, preferred_element_type=jnp.float32)
        grad_v = jnp.dot(windows_v.T, value_grad, preferred_element_type=jnp.float32)
        return (jnp.sum(differ * differ), grad_k, grad_v)
    losses, grad_k, grad_v = lax.map(recon_item, jnp.arange(N_SEG * H, dtype=jnp.int32))
    grad_conv_keys = lax.optimization_barrier(jnp.sum(grad_k.reshape(N_SEG, H, RATE * DH, DH), axis=0))
    grad_conv_values = lax.optimization_barrier(jnp.sum(grad_v.reshape(N_SEG, H, RATE * DH, DH), axis=0))
    recon_loss = jnp.sum(losses) / (N_SEG * SEG_LEN)
    compressed_keys = comp_keys.transpose(0, 2, 1, 3).reshape(N_SEG * COMP_ROWS, H * DH)
    compressed_values = comp_values.transpose(0, 2, 1, 3).reshape(N_SEG * COMP_ROWS, H * DH)
    return (attended, compressed_keys, compressed_values, recon_loss, grad_conv_keys, grad_conv_values)
```

```python
import functools
import math

import jax
import jax.numpy as jnp
from jax import lax
from jax.experimental import pallas as pl
from jax.experimental.pallas import tpu as pltpu
from jax.sharding import PartitionSpec as P

RATE = 4
HIDDEN = -1e30
BOTH = ("seg", "seq")


def on_vmem(limit_mib=60):
    return pltpu.CompilerParams(vmem_limit_bytes=limit_mib * 2**20)


def pack_kernel(rows, share, where_ref, q_ref, k_ref, v_ref, pk_ref, pv_ref, out_ref):
    del where_ref
    width = out_ref.shape[-1]
    for r in range(out_ref.shape[0]):
        columns = slice(r * width, (r + 1) * width)
        out_ref[r, 0, 0:rows, :] = q_ref[:, columns]
        out_ref[r, 0, rows : 2 * rows, :] = k_ref[:, columns]
        out_ref[r, 0, 2 * rows : 3 * rows, :] = v_ref[:, columns]
        out_ref[r, 0, 3 * rows : 3 * rows + share, :] = pk_ref[:, columns]
        out_ref[r, 0, 3 * rows + share :, :] = pv_ref[:, columns]


def pack(seg_at, queries, keys, values, prior_keys, prior_values, seg_count, seq_count):
    rows, columns = queries.shape
    share = rows // seg_count
    block = 3 * rows + 2 * share
    wide = columns // seq_count
    width = wide // seg_count
    whole = pl.BlockSpec((rows, wide), lambda s, at: (0, s))
    part = pl.BlockSpec((share, wide), lambda s, at: (at[0], s))
    return pl.pallas_call(
        functools.partial(pack_kernel, rows, share),
        out_shape=jax.ShapeDtypeStruct((seg_count, seq_count, block, width), queries.dtype),
        grid_spec=pltpu.PrefetchScalarGridSpec(
            num_scalar_prefetch=1,
            grid=(seq_count,),
            in_specs=[whole, whole, whole, part, part],
            out_specs=pl.BlockSpec((seg_count, 1, block, width), lambda s, at: (0, s, 0, 0)),
        ),
        compiler_params=on_vmem(),
        name="pack",
    )(seg_at, queries, keys, values, prior_keys, prior_values)


def unpack_kernel(in_ref, out_ref):
    width = in_ref.shape[-1]
    for r in range(in_ref.shape[0]):
        out_ref[:, r * width : (r + 1) * width] = in_ref[r, 0]


def unpack(blocks):
    seg_count, seq_count, rows, width = blocks.shape
    return pl.pallas_call(
        unpack_kernel,
        out_shape=jax.ShapeDtypeStruct((rows, seg_count * seq_count * width), blocks.dtype),
        grid=(seq_count,),
        in_specs=[pl.BlockSpec((seg_count, 1, rows, width), lambda s: (0, s, 0, 0))],
        out_specs=pl.BlockSpec((rows, seg_count * width), lambda s: (0, s)),
        compiler_params=on_vmem(),
        name="unpack",
    )(blocks)


def matmul_t(a, b):
    return lax.dot_general(a, b, (((1,), (1,)), ((), ())), preferred_element_type=jnp.float32)


def t_matmul(a, b):
    return lax.dot_general(a, b, (((0,), (0,)), ((), ())), preferred_element_type=jnp.float32)


def matmul(a, b):
    return jnp.dot(a, b, preferred_element_type=jnp.float32)


def mixed(scores, rate, values_and_ones):
    top = jnp.max(scores, axis=1, keepdims=True)
    weights = jnp.exp2((scores - top) * rate).astype(jnp.bfloat16)
    return top, matmul(weights, values_and_ones)


def attend_kernel(
    dims,
    starts_ref, at_ref, recv_ref, prior_ref, conv_k_ref, conv_v_ref,
    out_ref, recon_ref, comp_k_ref, comp_v_ref, win_k_ref, win_v_ref,
    fine_k, fine_v, cat_k, cat_v, rows_f32,
):
    rows, share, seg_count, seq_count, step = dims
    g = pl.program_id(0)
    seg_rows = rows * seq_count
    comp_rows = seg_rows // RATE
    width = recv_ref.shape[-1]
    rate = math.log2(math.e) / math.sqrt(width)
    bf16 = jnp.bfloat16

    @pl.when(g == 0)
    def _():
        cat_k[0:comp_rows, :] = jnp.zeros((comp_rows, width), bf16)
        cat_v[0:comp_rows, 0:width] = jnp.zeros((comp_rows, width), bf16)
        cat_v[:, width:] = jnp.ones((comp_rows + seg_rows, width), bf16)
        fine_v[:, width:] = jnp.ones((seg_rows, width), bf16)
        for s in range(seq_count):
            for i in range(seg_count):
                at = s * rows + i * share
                fine_k[at : at + share, :] = prior_ref[i, s, 0:share, :]
                fine_v[at : at + share, 0:width] = prior_ref[i, s, share:, :]

    @pl.when(g > 0)
    def _():
        fine_k[...] = cat_k[comp_rows:, :]
        fine_v[:, 0:width] = cat_v[comp_rows:, 0:width]

    own_k = recv_ref[0, :, rows : 2 * rows, :].reshape(seg_rows, width)
    own_v = recv_ref[0, :, 2 * rows : 3 * rows, :].reshape(seg_rows, width)
    cat_k[comp_rows:, :] = own_k
    cat_v[comp_rows:, 0:width] = own_v

    for fine, conv, comp, win in (
        (fine_k, conv_k_ref, comp_k_ref, win_k_ref),
        (fine_v, conv_v_ref, comp_v_ref, win_v_ref),
    ):
        rows_f32[...] = fine[:, 0:width].astype(jnp.float32)
        for r in range(RATE):
            win[0, :, r * width : (r + 1) * width] = rows_f32[
                pl.ds(r, comp_rows, stride=RATE), :
            ].astype(bf16)
        comp[0] = matmul(win[0], conv[0]).astype(bf16)

    def start_of(i):
        return jnp.where(i >= 0, starts_ref[jnp.maximum(i, 0)], seg_rows)

    b0, b1, b2 = start_of(g), start_of(g - 1), start_of(g - 2)
    s1 = jnp.where(b1 < seg_rows, b1, 0)
    s2 = jnp.where(b2 < seg_rows, b2, 0)
    memory_from = jnp.where((g >= 1) & (b1 >= seg_rows), s2, RATE * comp_rows)

    def attend(doc, fine_from_s1):
        for p0 in range(0, seg_rows, step):
            blocks = slice(p0 // rows, (p0 + step) // rows)
            q = recv_ref[0, blocks, 0:rows, :].reshape(step, width)
            fine_scores = matmul_t(q, fine_k[...])
            fine_top, fine_mix = mixed(fine_scores, rate, fine_v[...])
            recon_ref[p0 : p0 + step, :] = fine_mix[:, 0:width] / fine_mix[:, width:]
            if fine_from_s1:
                place = lax.broadcasted_iota(jnp.int32, (step, seg_rows), 1)
                fine_top, fine_mix = mixed(
                    jnp.where(place >= s1, fine_scores, HIDDEN), rate, fine_v[...]
                )

            seen = comp_rows + p0 + step
            scores = matmul_t(q, cat_k[0:seen, :])
            place_q = p0 + lax.broadcasted_iota(jnp.int32, (step, comp_rows), 0)
            place_k = RATE * lax.broadcasted_iota(jnp.int32, (step, comp_rows), 1)
            memory_seen = place_k >= memory_from
            if doc:
                memory_seen &= place_q < b0
            parts = [jnp.where(memory_seen, scores[:, 0:comp_rows], HIDDEN)]
            if doc:
                place_q = p0 + lax.broadcasted_iota(jnp.int32, (step, p0 + step), 0)
                place_k = lax.broadcasted_iota(jnp.int32, (step, p0 + step), 1)
                own_seen = (place_k <= place_q) & ((place_k >= b0) | (place_q < b0))
                parts.append(jnp.where(own_seen, scores[:, comp_rows:], HIDDEN))
            else:
                if p0:
                    parts.append(scores[:, comp_rows : comp_rows + p0])
                place_q = lax.broadcasted_iota(jnp.int32, (step, step), 0)
                place_k = lax.broadcasted_iota(jnp.int32, (step, step), 1)
                parts.append(jnp.where(place_k <= place_q, scores[:, comp_rows + p0 :], HIDDEN))
            top, mix = mixed(jnp.concatenate(parts, axis=1), rate, cat_v[0:seen, :])

            both_top = jnp.maximum(top, fine_top)
            if doc:
                before = p0 + lax.broadcasted_iota(jnp.int32, (step, 1), 0) < b0
                both_top = jnp.where(before, both_top, top)
                fine_share = jnp.where(before, jnp.exp2((fine_top - both_top) * rate), 0.0)
            else:
                fine_share = jnp.exp2((fine_top - both_top) * rate)
            share_own = jnp.exp2((top - both_top) * rate)
            total = mix * share_own + fine_mix * fine_share
            out_ref[p0 : p0 + step, :] = (total[:, 0:width] / total[:, width:]).astype(bf16)

    @pl.when((b0 >= seg_rows) & (s1 <= 0))
    def _():
        attend(False, False)

    @pl.when((b0 < seg_rows) & (s1 <= 0))
    def _():
        attend(True, False)

    @pl.when(s1 > 0)
    def _():
        attend(True, True)

    cat_k[0:comp_rows, :] = comp_k_ref[0]
    cat_v[0:comp_rows, 0:width] = comp_v_ref[0]


def attend_all(starts, seg_at, recv, conv_keys, conv_values, share):
    seg_count, seq_count, block, width = recv.shape
    rows = (block - 2 * share) // 3
    seg_rows = rows * seq_count
    comp_rows = seg_rows // RATE
    step = math.gcd(seg_rows, 256)
    dims = (rows, share, seg_count, seq_count, step)
    bf16 = jnp.bfloat16
    shape = jax.ShapeDtypeStruct
    per_seg = lambda g, starts, at: (g, 0, 0)
    conv = pl.BlockSpec((1, RATE * width, width), lambda g, starts, at: (at[0], 0, 0))
    return pl.pallas_call(
        functools.partial(attend_kernel, dims),
        out_shape=(
            shape((seg_count * seg_rows, width), bf16),
            shape((seg_count * seg_rows, width), jnp.float32),
            shape((seg_count, comp_rows, width), bf16),
            shape((seg_count, comp_rows, width), bf16),
            shape((seg_count, comp_rows, RATE * width), bf16),
            shape((seg_count, comp_rows, RATE * width), bf16),
        ),
        grid_spec=pltpu.PrefetchScalarGridSpec(
            num_scalar_prefetch=2,
            grid=(seg_count,),
            in_specs=[
                pl.BlockSpec((1, seq_count, block, width), lambda g, starts, at: (g, 0, 0, 0)),
                pl.BlockSpec(
                    (seg_count, seq_count, 2 * share, width),
                    lambda g, starts, at: (0, 0, 3 * rows // (2 * share), 0),
                ),
                conv,
                conv,
            ],
            out_specs=(
                pl.BlockSpec((seg_rows, width), lambda g, starts, at: (g, 0)),
                pl.BlockSpec((seg_rows, width), lambda g, starts, at: (g, 0)),
                pl.BlockSpec((1, comp_rows, width), per_seg),
                pl.BlockSpec((1, comp_rows, width), per_seg),
                pl.BlockSpec((1, comp_rows, RATE * width), per_seg),
                pl.BlockSpec((1, comp_rows, RATE * width), per_seg),
            ),
            scratch_shapes=[
                pltpu.VMEM((seg_rows, width), bf16),
                pltpu.VMEM((seg_rows, 2 * width), bf16),
                pltpu.VMEM((comp_rows + seg_rows, width), bf16),
                pltpu.VMEM((comp_rows + seg_rows, 2 * width), bf16),
                pltpu.VMEM((seg_rows, width), jnp.float32),
            ],
        ),
        compiler_params=on_vmem(),
        cost_estimate=pl.CostEstimate(
            flops=16 * seg_count * seg_rows * seg_rows * width, bytes_accessed=2**23, transcendentals=0
        ),
        name="attend",
    )(starts, seg_at, recv, recv, conv_keys, conv_values)


def recon_kernel(
    dims, recv_ref, recon_ref, comp_k_ref, comp_v_ref, win_k_ref, win_v_ref,
    grad_ref, loss_ref, sums, losses,
):
    rows, seq_count = dims
    g = pl.program_id(0)
    width = recv_ref.shape[-1]
    seg_rows = rows * seq_count
    scale = 1.0 / math.sqrt(width)
    rate = math.log2(math.e) * scale
    bf16 = jnp.bfloat16

    @pl.when(g == 0)
    def _():
        sums[...] = jnp.zeros_like(sums)
        losses[...] = jnp.zeros_like(losses)

    q = recv_ref[0, :, 0:rows, :].reshape(seg_rows, width)
    comp_k, comp_v = comp_k_ref[0], comp_v_ref[0]
    scores = matmul_t(q, comp_k)
    top = jnp.max(scores, axis=1, keepdims=True)
    comp_exp = jnp.exp2((scores - top) * rate)
    total = jnp.sum(comp_exp, axis=1, keepdims=True)
    weights = comp_exp.astype(bf16)
    recon_comp = matmul(weights, comp_v) / total
    differ = recon_ref[...] - recon_comp
    losses[...] += jnp.sum(differ * differ, axis=0, keepdims=True)
    out_grad = (-2.0 * differ / total).astype(bf16)
    value_rows = t_matmul(weights, out_grad).astype(bf16)
    inner = matmul_t(out_grad, comp_v)
    offset = jnp.sum(out_grad.astype(jnp.float32) * recon_comp, axis=1, keepdims=True)
    score_grad = (comp_exp * (inner - offset)).astype(bf16)
    key_rows = (t_matmul(score_grad, q) * scale).astype(bf16)
    sums[0] += t_matmul(win_k_ref[0], key_rows)
    sums[1] += t_matmul(win_v_ref[0], value_rows)

    @pl.when(g == pl.num_programs(0) - 1)
    def _():
        grad_ref[...] = sums[...].astype(bf16)
        loss_ref[...] = jnp.broadcast_to(jnp.sum(losses[...], keepdims=True), loss_ref.shape)


def recon_all(recv, recon, comp_k, comp_v, win_k, win_v, rows):
    seg_count, seq_count, block, width = recv.shape
    seg_rows = rows * seq_count
    comp_rows = seg_rows // RATE
    per_seg = lambda g: (g, 0, 0)
    return pl.pallas_call(
        functools.partial(recon_kernel, (rows, seq_count)),
        out_shape=(
            jax.ShapeDtypeStruct((2, RATE * width, width), jnp.bfloat16),
            jax.ShapeDtypeStruct((8, width), jnp.float32),
        ),
        grid=(seg_count,),
        in_specs=[
            pl.BlockSpec((1, seq_count, block, width), lambda g: (g, 0, 0, 0)),
            pl.BlockSpec((seg_rows, width), lambda g: (g, 0)),
            pl.BlockSpec((1, comp_rows, width), per_seg),
            pl.BlockSpec((1, comp_rows, width), per_seg),
            pl.BlockSpec((1, comp_rows, RATE * width), per_seg),
            pl.BlockSpec((1, comp_rows, RATE * width), per_seg),
        ],
        out_specs=(
            pl.BlockSpec((2, RATE * width, width), lambda g: (0, 0, 0)),
            pl.BlockSpec((8, width), lambda g: (0, 0)),
        ),
        scratch_shapes=[
            pltpu.VMEM((2, RATE * width, width), jnp.float32),
            pltpu.VMEM((1, width), jnp.float32),
        ],
        compiler_params=on_vmem(),
        cost_estimate=pl.CostEstimate(
            flops=4 * seg_count * seg_rows * seg_rows * width, bytes_accessed=2**22, transcendentals=0
        ),
        name="recon",
    )(recv, recon, comp_k, comp_v, win_k, win_v)


def gather_kernel(at_ref, in_ref, k_ref, v_ref):
    del at_ref
    k_ref[...] = in_ref[0, 0, 0]
    v_ref[...] = in_ref[0, 0, 1]


def comp_outputs(seg_at, comp_k, comp_v):
    seg_count, comp_rows, width = comp_k.shape
    me = seg_at[0]
    both = jnp.stack((comp_k, comp_v), axis=1)
    arrived = []
    for step in range(seg_count):
        to = lax.rem(me + step, seg_count)
        part = lax.dynamic_slice_in_dim(both, to, 1, 0)
        if step:
            route = [(i, (i + step) % seg_count) for i in range(seg_count)]
            part = lax.ppermute(part, "seg", route)
        arrived.append(part)
    arrived = jnp.stack(arrived)
    shape = jax.ShapeDtypeStruct((comp_rows, seg_count * width), comp_k.dtype)
    return pl.pallas_call(
        gather_kernel,
        out_shape=(shape, shape),
        grid_spec=pltpu.PrefetchScalarGridSpec(
            num_scalar_prefetch=1,
            grid=(seg_count,),
            in_specs=[
                pl.BlockSpec(
                    (1, 1, 2, comp_rows, width),
                    lambda h, at: (lax.rem(at[0] - h + seg_count, seg_count), 0, 0, 0, 0),
                )
            ],
            out_specs=[pl.BlockSpec((comp_rows, width), lambda h, at: (0, h))] * 2,
        ),
        compiler_params=on_vmem(),
        name="comp_columns",
    )(seg_at, arrived)


def head_on_device(
    queries, keys, values, prior_keys, prior_values, conv_keys, conv_values, doc_starts
):
    seq_count = lax.axis_size("seq")
    seg_count = lax.axis_size("seg")
    rows = queries.shape[0]
    share = rows // seg_count
    width = conv_keys.shape[2]
    seg_at = lax.axis_index("seg").astype(jnp.int32).reshape(1)

    packed = pack(
        seg_at, queries, keys, values, prior_keys, prior_values, seg_count, seq_count
    )
    block = packed.shape[2]
    recv = lax.all_to_all(
        packed.reshape(seg_count * seq_count, block, width), BOTH, split_axis=0, concat_axis=0, tiled=True
    ).reshape(packed.shape)
    attended, recon, comp_k, comp_v, win_k, win_v = attend_all(
        doc_starts, seg_at, recv, conv_keys, conv_values, share
    )
    attended = lax.all_to_all(
        attended.reshape(seg_count * seq_count, rows, width), BOTH, split_axis=0, concat_axis=0, tiled=True
    ).reshape(seg_count, seq_count, rows, width)
    attended = unpack(attended)
    grads, loss = recon_all(recv, recon, comp_k, comp_v, win_k, win_v, rows)
    comp_keys, comp_values = comp_outputs(seg_at, comp_k, comp_v)
    grads = lax.all_gather(grads, "seg").astype(jnp.float32)
    for axis, count in (("seq", seq_count), ("seg", seg_count)):
        bit = 1
        while bit < count:
            loss = loss + lax.ppermute(loss, axis, [(i, i ^ bit) for i in range(count)])
            bit *= 2
    recon_loss = loss[0, 0] / (seg_count * rows * seq_count)
    return (attended, comp_keys, comp_values, recon_loss, grads[:, 0], grads[:, 1])


def shifted_2(block, axis, distance):
    devices = range(lax.axis_size(axis))
    route = [(i - distance, i) for i in devices if i - distance in devices]
    return lax.ppermute(block, axis, route)


def pick_entry(small_table, wanted):
    return jnp.sum(jnp.where(jnp.arange(small_table.shape[0]) == wanted, small_table, 0))


def compress(source_rows, weight):
    head_count = weight.shape[0]
    head_width = weight.shape[2]
    windows = source_rows.reshape(source_rows.shape[0] // RATE, RATE, head_count, head_width)
    kernel = weight.reshape(head_count, RATE, head_width, head_width)
    merged = jnp.einsum("crhd,hrde->che", windows, kernel, preferred_element_type=jnp.float32)
    return merged.reshape(merged.shape[0], head_count * head_width).astype(jnp.bfloat16)


def on_device(queries, keys, values, prior_keys, prior_values, conv_keys, conv_values, doc_starts):
    seq_count = lax.axis_size("seq")
    seg_count = lax.axis_size("seg")
    group_index = lax.axis_index("seg")
    seg_rows = queries.shape[0] * seq_count
    head_count = conv_keys.shape[0]
    head_width = conv_keys.shape[2]
    comp_rows = seg_rows // RATE
    score_scale = 1.0 / math.sqrt(head_width)
    first_group = group_index == 0
    shifted = shifted_2(jnp.stack((keys, values)), "seg", 1)
    previous = jnp.where(first_group, jnp.stack((prior_keys, prior_values)), shifted)
    moved = (
        lax.all_to_all(queries, "seq", split_axis=1, concat_axis=0, tiled=True),
        lax.all_to_all(keys, "seq", split_axis=1, concat_axis=0, tiled=True),
        lax.all_to_all(values, "seq", split_axis=1, concat_axis=0, tiled=True),
        lax.all_to_all(previous[0], "seq", split_axis=1, concat_axis=0, tiled=True),
        lax.all_to_all(previous[1], "seq", split_axis=1, concat_axis=0, tiled=True),
    )
    query_heads = moved[0]
    key_heads = moved[1]
    value_heads = moved[2]
    fine_keys = moved[3]
    fine_values = moved[4]
    comp_keys = compress(fine_keys, conv_keys)
    comp_values = compress(fine_values, conv_values)
    memory = shifted_2(jnp.stack((comp_keys, comp_values)), "seg", 1)
    start_now = pick_entry(doc_starts, group_index)
    start_prev = jnp.where(group_index >= 1, pick_entry(doc_starts, group_index - 1), seg_rows)
    start_back = jnp.where(group_index >= 2, pick_entry(doc_starts, group_index - 2), seg_rows)
    lead_prev = jnp.where(start_prev < seg_rows, start_prev, 0)
    lead_back = jnp.where(start_back < seg_rows, start_back, 0)
    comp_open = (group_index >= 1) & (start_prev >= seg_rows)
    all_keys = jnp.concatenate((memory[0], fine_keys, key_heads), axis=0)
    all_values = jnp.concatenate((memory[1], fine_values, value_heads), axis=0)
    block_rows = math.gcd(seg_rows, 512)
    block_count = seg_rows // block_rows
    column = jnp.arange(comp_rows + 2 * seg_rows, dtype=jnp.int32)[None, :]
    comp_part = column < comp_rows
    fine_part = (column >= comp_rows) & (column < comp_rows + seg_rows)
    own_part = column >= comp_rows + seg_rows
    key_place = jnp.where(
        comp_part,
        RATE * column,
        jnp.where(fine_part, column - comp_rows, column - comp_rows - seg_rows),
    )

    def attend_block(flat_index):
        head_index = flat_index // block_count
        block_index = flat_index % block_count
        query_block = lax.dynamic_slice(
            query_heads,
            (block_index * block_rows, head_index * head_width),
            (block_rows, head_width),
        )
        key_block = lax.dynamic_slice_in_dim(all_keys, head_index * head_width, head_width, 1)
        value_block = lax.dynamic_slice_in_dim(all_values, head_index * head_width, head_width, 1)
        scores = (
            jnp.einsum("qd,kd->qk", query_block, key_block, preferred_element_type=jnp.float32)
            * score_scale
        )
        query_place = block_index * block_rows + jnp.arange(block_rows, dtype=jnp.int32)[:, None]
        before_doc = query_place < start_now
        seen_comp = comp_part & comp_open & before_doc & (key_place >= lead_back)
        seen_fine = fine_part & before_doc & (key_place >= lead_prev)
        seen_own = own_part & (key_place <= query_place) & ((key_place >= start_now) | before_doc)
        visible = seen_comp | seen_fine | seen_own
        row_top = jnp.max(jnp.where(visible, scores, -jnp.inf), axis=1, keepdims=True)
        weights = jnp.exp(jnp.where(visible, scores - row_top, -jnp.inf))
        row_total = jnp.sum(weights, axis=1, keepdims=True)
        mixed_rows = (
            jnp.dot(weights.astype(jnp.bfloat16), value_block, preferred_element_type=jnp.float32)
            / row_total
        )
        return mixed_rows.astype(jnp.bfloat16)

    pieces = lax.map(attend_block, jnp.arange(head_count * block_count, dtype=jnp.int32))
    attended_heads = (
        pieces.reshape(head_count, seg_rows, head_width)
        .transpose(1, 0, 2)
        .reshape(seg_rows, head_count * head_width)
    )
    attended = lax.all_to_all(attended_heads, "seq", split_axis=0, concat_axis=1, tiled=True)

    def recon_head(head_index):
        start_col = head_index * head_width
        query_full = lax.dynamic_slice_in_dim(query_heads, start_col, head_width, 1)
        fine_k = lax.dynamic_slice_in_dim(fine_keys, start_col, head_width, 1)
        fine_v = lax.dynamic_slice_in_dim(fine_values, start_col, head_width, 1)
        comp_k = lax.dynamic_slice_in_dim(comp_keys, start_col, head_width, 1)
        comp_v = lax.dynamic_slice_in_dim(comp_values, start_col, head_width, 1)

        def recon_step(running, block_index):
            loss_sum, value_acc, key_acc = running
            query_block = lax.dynamic_slice_in_dim(
                query_full, block_index * block_rows, block_rows, 0
            )
            fine_scores = (
                jnp.einsum("qd,kd->qk", query_block, fine_k, preferred_element_type=jnp.float32)
                * score_scale
            )
            fine_exp = jnp.exp(fine_scores - jnp.max(fine_scores, axis=1, keepdims=True))
            fine_total = jnp.sum(fine_exp, axis=1, keepdims=True)
            recon_fine = (
                jnp.dot(fine_exp.astype(jnp.bfloat16), fine_v, preferred_element_type=jnp.float32)
                / fine_total
            )
            comp_scores = (
                jnp.einsum("qd,kd->qk", query_block, comp_k, preferred_element_type=jnp.float32)
                * score_scale
            )
            comp_exp = jnp.exp(comp_scores - jnp.max(comp_scores, axis=1, keepdims=True))
            comp_total = jnp.sum(comp_exp, axis=1, keepdims=True)
            comp_weights = comp_exp.astype(jnp.bfloat16)
            recon_comp = (
                jnp.dot(comp_weights, comp_v, preferred_element_type=jnp.float32) / comp_total
            )
            differ = recon_fine - recon_comp
            out_grad = (-2.0 * differ / comp_total).astype(jnp.bfloat16)
            value_acc = value_acc + jnp.einsum(
                "qc,qd->cd", comp_weights, out_grad, preferred_element_type=jnp.float32
            )
            inner_grad = jnp.einsum(
                "qd,cd->qc", out_grad, comp_v, preferred_element_type=jnp.float32
            )
            row_offset = jnp.sum(out_grad.astype(jnp.float32) * recon_comp, axis=1, keepdims=True)
            score_grad = (comp_exp * (inner_grad - row_offset)).astype(jnp.bfloat16)
            key_acc = key_acc + jnp.einsum(
                "qc,qd->cd", score_grad, query_block, preferred_element_type=jnp.float32
            )
            return ((loss_sum + jnp.sum(differ * differ), value_acc, key_acc), None)

        zero_rows = jnp.zeros((comp_rows, head_width), jnp.float32)
        start_state = (jnp.zeros((), jnp.float32), zero_rows, zero_rows)
        (loss_sum, value_acc, key_acc), unused = lax.scan(
            recon_step, start_state, jnp.arange(block_count, dtype=jnp.int32)
        )
        key_grad = (key_acc * score_scale).astype(jnp.bfloat16)
        value_grad = value_acc.astype(jnp.bfloat16)
        windows_k = fine_k.reshape(comp_rows, RATE * head_width)
        windows_v = fine_v.reshape(comp_rows, RATE * head_width)
        grad_k = jnp.einsum("cw,cd->wd", windows_k, key_grad, preferred_element_type=jnp.float32)
        grad_v = jnp.einsum("cw,cd->wd", windows_v, value_grad, preferred_element_type=jnp.float32)
        return (loss_sum, grad_k, grad_v)

    losses, grad_k, grad_v = lax.map(recon_head, jnp.arange(head_count, dtype=jnp.int32))
    grad_k, grad_v = (
        lax.psum(grad_k.astype(jnp.bfloat16), "seg").astype(jnp.float32),
        lax.psum(grad_v.astype(jnp.bfloat16), "seg").astype(jnp.float32),
    )
    total_loss = lax.psum(jnp.sum(losses), ("seg", "seq"))
    recon_loss = total_loss / (seg_count * seg_rows)
    return (attended, comp_keys, comp_values, recon_loss, grad_k, grad_v)


def solution(mesh):
    def body(*arrays):
        heads, width = arrays[5].shape[0], arrays[5].shape[2]
        rows = arrays[0].shape[0]
        by_head = heads == mesh.shape["seg"] and width % 128 == 0
        by_head = by_head and all(n & (n - 1) == 0 for n in mesh.shape.values())
        by_head = by_head and heads % 2 == 0 and rows % (16 * heads) == 0 and 256 % rows == 0
        return (head_on_device if by_head else on_device)(*arrays)

    return jax.shard_map(
        body,
        mesh=mesh,
        in_specs=(
            P(("seg", "seq"), None),
            P(("seg", "seq"), None),
            P(("seg", "seq"), None),
            P("seq", None),
            P("seq", None),
            P("seq", None, None),
            P("seq", None, None),
            P(),
        ),
        out_specs=(
            P(("seg", "seq"), None),
            P("seg", "seq"),
            P("seg", "seq"),
            P(),
            P("seq", None, None),
            P("seq", None, None),
        ),
        check_vma=False,
    )
```

```python
import functools
import math

import jax
import jax.numpy as jnp
from jax import lax
from jax.experimental import pallas as pl
from jax.experimental.pallas import tpu as pltpu
from jax.sharding import PartitionSpec as P

RATE = 4
HIDDEN = -1e30
BOTH = ("seg", "seq")


def on_vmem(limit_mib=60):
    return pltpu.CompilerParams(vmem_limit_bytes=limit_mib * 2**20)


def pack_kernel(at_ref, *refs):
    del at_ref
    out_ref = refs[-1]
    seg_count, seq_count, _, width = out_ref.shape
    for s in range(seq_count):
        for r in range(seg_count):
            column = (s * seg_count + r) * width
            row = 0
            for ref in refs[:-1]:
                rows = ref.shape[0]
                out_ref[r, s, row : row + rows, :] = ref[:, column : column + width]
                row += rows


def pack(at, arrays, prior_arrays, seg_count, seq_count):
    rows, columns = arrays[0].shape
    width = columns // (seg_count * seq_count)
    share = rows // seg_count
    block = len(arrays) * rows + len(prior_arrays) * share
    steps = 2
    wide = columns // steps
    return pl.pallas_call(
        pack_kernel,
        out_shape=jax.ShapeDtypeStruct((seg_count, seq_count, block, width), arrays[0].dtype),
        grid_spec=pltpu.PrefetchScalarGridSpec(
            num_scalar_prefetch=1,
            grid=(steps,),
            in_specs=[
                *[pl.BlockSpec((rows, wide), lambda s, at: (0, s))] * len(arrays),
                *[pl.BlockSpec((share, wide), lambda s, at: (at[0], s))] * len(prior_arrays),
            ],
            out_specs=pl.BlockSpec(
                (seg_count, seq_count // steps, block, width), lambda s, at: (0, s, 0, 0)
            ),
        ),
        compiler_params=on_vmem(),
        name="pack",
    )(at, *arrays, *prior_arrays)


def unpack_kernel(positions, in_ref, out_ref, loss_ref, rows_ref, tails, sems):
    seg_count, seq_count, _, width = in_ref.shape
    rows = rows_ref.shape[0]
    copies = []
    for s in range(seq_count):
        for r in range(seg_count):
            at = s * seg_count + r
            columns = slice(at * width, (at + 1) * width)
            from_ref = in_ref.at[r, s, 0:rows, :]
            copies.append(pltpu.make_async_copy(from_ref, rows_ref.at[:, columns], sems.at[at]))
            copies[-1].start()
    spare = tails.shape[2]
    tail = pltpu.make_async_copy(
        in_ref.at[:, :, rows : rows + spare, :], tails, sems.at[seg_count * seq_count]
    )
    tail.start()
    for copy in copies:
        copy.wait()
    copy = pltpu.make_async_copy(rows_ref, out_ref, sems.at[seg_count * seq_count + 1])
    copy.start()
    tail.wait()
    parts = tails[...].reshape(-1, width).astype(jnp.float32)
    total = jnp.sum(jnp.sum(parts, axis=0, keepdims=True), axis=1, keepdims=True)
    loss_ref[...] = total / positions
    copy.wait()


def unpack(blocks, rows, positions):
    seg_count, seq_count, _, width = blocks.shape
    spare = blocks.shape[2] - rows
    shape = (rows, seg_count * seq_count * width)
    return pl.pallas_call(
        functools.partial(unpack_kernel, positions),
        out_shape=(
            jax.ShapeDtypeStruct(shape, blocks.dtype),
            jax.ShapeDtypeStruct((1, 1), jnp.float32),
        ),
        in_specs=[pl.BlockSpec(memory_space=pl.ANY)],
        out_specs=(
            pl.BlockSpec(memory_space=pl.ANY),
            pl.BlockSpec(memory_space=pltpu.VMEM),
        ),
        scratch_shapes=[
            pltpu.VMEM(shape, blocks.dtype),
            pltpu.VMEM((seg_count, seq_count, spare, width), blocks.dtype),
            pltpu.SemaphoreType.DMA((seg_count * seq_count + 2,)),
        ],
        compiler_params=on_vmem(8),
        name="unpack",
    )(blocks)


def matmul_t(a, b):
    return lax.dot_general(a, b, (((1,), (1,)), ((), ())), preferred_element_type=jnp.float32)


def t_matmul(a, b):
    return lax.dot_general(a, b, (((0,), (0,)), ((), ())), preferred_element_type=jnp.float32)


def matmul(a, b):
    return jnp.dot(a, b, preferred_element_type=jnp.float32)


def softmax_part(scores, rate):
    top = jnp.max(scores, axis=1, keepdims=True)
    return top, jnp.exp2((scores - top) * rate)


def merge_taps(fine, conv, comp, win, rows_f32):
    comp_rows, width = comp.shape
    rows_f32[...] = fine[:, 0:width].astype(jnp.float32)
    for r in range(RATE):
        taps = rows_f32[pl.ds(r, comp_rows, stride=RATE), :]
        win[:, r * width : (r + 1) * width] = taps.astype(jnp.bfloat16)
    comp[...] = matmul(win[...], conv[0]).astype(jnp.bfloat16)


def doc_bounds(starts_ref, g, seg_rows, comp_rows):
    def start_of(i):
        return jnp.where(i >= 0, starts_ref[jnp.maximum(i, 0)], seg_rows)

    b0, b1, b2 = start_of(g), start_of(g - 1), start_of(g - 2)
    s1 = jnp.where(b1 < seg_rows, b1, 0)
    s2 = jnp.where(b2 < seg_rows, b2, 0)
    memory_from = jnp.where((g >= 1) & (b1 >= seg_rows), s2, RATE * comp_rows)
    return b0, s1, memory_from


def memory_scores(scores, p0, b0, memory_from):
    place_q = p0 + lax.broadcasted_iota(jnp.int32, scores.shape, 0)
    place_k = RATE * lax.broadcasted_iota(jnp.int32, scores.shape, 1)
    return jnp.where((place_q < b0) & (place_k >= memory_from), scores, HIDDEN)


def own_scores(scores, p0, b0):
    place_q = p0 + lax.broadcasted_iota(jnp.int32, scores.shape, 0)
    place_k = lax.broadcasted_iota(jnp.int32, scores.shape, 1)
    seen = (place_k <= place_q) & ((place_k >= b0) | (place_q < b0))
    return jnp.where(seen, scores, HIDDEN)


def before_doc(step, p0, b0):
    return p0 + lax.broadcasted_iota(jnp.int32, (step, 1), 0) < b0


def head_kernel(
    dims, starts_ref, at_ref, recv_ref, prior_ref, conv_k_ref, conv_v_ref,
    out_ref, *rest,
):
    rows, seq_count, step = dims
    share_refs, rest = rest[: prior_ref.shape[0]], rest[prior_ref.shape[0] :]
    (
        out_rows, loss_rows, comp_ref, fine_k, fine_v, cat_k, cat_v, rows_f32,
        win_k, win_v, comp_w, out_grads, score_grads, sums, losses, sems,
    ) = rest
    g = pl.program_id(0)
    seg_rows = rows * seq_count
    comp_rows = seg_rows // RATE
    seg_count, _, both_shares, width = prior_ref.shape
    share = both_shares // 2
    scale = 1.0 / math.sqrt(width)
    rate = math.log2(math.e) * scale
    bf16 = jnp.bfloat16

    @pl.when(g == 0)
    def _():
        cat_k[0:comp_rows, :] = jnp.zeros((comp_rows, width), bf16)
        cat_v[0:comp_rows, 0:width] = jnp.zeros((comp_rows, width), bf16)
        cat_v[:, width:] = jnp.ones((comp_rows + seg_rows, width), bf16)
        fine_v[:, width:] = jnp.ones((seg_rows, width), bf16)
        sums[...] = jnp.zeros_like(sums)
        losses[...] = jnp.zeros_like(losses)
        for s in range(seq_count):
            for i in range(seg_count):
                at = s * rows + i * share
                fine_k[at : at + share, :] = prior_ref[i, s, 0:share, :]
                fine_v[at : at + share, 0:width] = prior_ref[i, s, share:, :]

    @pl.when(g > 0)
    def _():
        fine_k[...] = cat_k[comp_rows:, :]
        fine_v[:, 0:width] = cat_v[comp_rows:, 0:width]

    cat_k[comp_rows:, :] = recv_ref[0, :, rows : 2 * rows, :].reshape(seg_rows, width)
    cat_v[comp_rows:, 0:width] = recv_ref[0, :, 2 * rows : 3 * rows, :].reshape(seg_rows, width)
    merge_taps(fine_k, conv_k_ref, comp_ref.at[0], win_k, rows_f32)
    merge_taps(fine_v, conv_v_ref, comp_ref.at[1], win_v, rows_f32)
    comp_k, comp_v = comp_ref[0], comp_ref[1]
    for i, share_ref in enumerate(share_refs):

        @pl.when(lax.rem(g - at_ref[0] + seg_count, seg_count) == i)
        def _():
            share_ref[0 : 2 * comp_rows, :] = comp_ref[...].reshape(2 * comp_rows, width)

    b0, s1, memory_from = doc_bounds(starts_ref, g, seg_rows, comp_rows)

    def queries(p0):
        return recv_ref[0, p0 // rows : (p0 + step) // rows, 0:rows, :].reshape(step, width)

    def weighted(weights, values_and_ones):
        mix = matmul(weights.astype(bf16), values_and_ones)
        return mix[:, 0:width], mix[:, width:]

    def attend(fine_from_s1):
        fine, recon = {}, {}

        def fine_scores(p0):
            return matmul_t(queries(p0), fine_k[...])

        def fine_part(p0, scores):
            top, weights = softmax_part(scores, rate)
            mix, total = weighted(weights, fine_v[...])
            recon[p0] = mix / total
            if fine_from_s1:
                place = lax.broadcasted_iota(jnp.int32, scores.shape, 1)
                top, weights = softmax_part(jnp.where(place >= s1, scores, HIDDEN), rate)
                mix, total = weighted(weights, fine_v[...])
            fine[p0] = top, mix, total

        def comp_scores(p0):
            return matmul_t(queries(p0), comp_k)

        def comp_part(p0, scores):
            here = slice(p0, p0 + step)
            _, comp_exp = softmax_part(scores, rate)
            total = jnp.sum(comp_exp, axis=1, keepdims=True)
            weights = comp_exp.astype(bf16)
            recon_comp = matmul(weights, comp_v) / total
            differ = recon.pop(p0) - recon_comp
            losses[...] += jnp.sum(differ * differ, axis=0, keepdims=True)
            out_grad = (-2.0 * differ / total).astype(bf16)
            inner = matmul_t(out_grad, comp_v)
            offset = jnp.sum(out_grad.astype(jnp.float32) * recon_comp, axis=1, keepdims=True)
            comp_w[here, :] = weights
            out_grads[here, :] = out_grad
            score_grads[here, :] = (comp_exp * (inner - offset)).astype(bf16)

        def cat_scores(p0):
            scores = matmul_t(queries(p0), cat_k[0 : comp_rows + p0 + step, :])
            memory = memory_scores(scores[:, 0:comp_rows], p0, b0, memory_from)
            return jnp.concatenate((memory, own_scores(scores[:, comp_rows:], p0, b0)), axis=1)

        def cat_part(p0, scores):
            top, weights = softmax_part(scores, rate)
            mix, total = weighted(weights, cat_v[0 : comp_rows + p0 + step, :])
            fine_top, fine_mix, fine_total = fine.pop(p0)
            seen = before_doc(step, p0, b0)
            both = jnp.where(seen, jnp.maximum(top, fine_top), top)
            fine_share = jnp.where(seen, jnp.exp2((fine_top - both) * rate), 0.0)
            cat_share = jnp.exp2((top - both) * rate)
            mix = mix * cat_share + fine_mix * fine_share
            total = total * cat_share + fine_total * fine_share
            here = slice(p0 // rows, (p0 + step) // rows)
            out_rows[g, here] = (mix / total).astype(bf16).reshape(step // rows, rows, width)

        parts = [
            (p0, *part)
            for p0 in range(0, seg_rows, step)
            for part in ((fine_scores, fine_part), (cat_scores, cat_part), (comp_scores, comp_part))
        ]
        ahead = parts[0][1](parts[0][0])
        for i, (p0, _, finish) in enumerate(parts):
            scores = ahead
            if i + 1 < len(parts):
                ahead = parts[i + 1][1](parts[i + 1][0])
            finish(p0, scores)

    @pl.when(s1 <= 0)
    def _():
        attend(False)

    @pl.when(s1 > 0)
    def _():
        attend(True)

    def copy_out(i):
        return pltpu.make_async_copy(out_rows.at[i], out_ref.at[i, :, 0:rows, :], sems.at[i])

    copy_out(g).start()
    cat_k[0:comp_rows, :] = comp_k
    cat_v[0:comp_rows, 0:width] = comp_v
    q = recv_ref[0, :, 0:rows, :].reshape(seg_rows, width)
    value_rows = t_matmul(comp_w[...], out_grads[...]).astype(bf16)
    key_rows = (t_matmul(score_grads[...], q) * scale).astype(bf16)
    sums[0] += t_matmul(win_k[...], key_rows)
    sums[1] += t_matmul(win_v[...], value_rows)

    @pl.when(g == seg_count - 1)
    def _():
        left = losses[...]
        parts = []
        for _ in range(3):
            parts.append(left.astype(bf16).astype(jnp.float32))
            left = left - parts[-1]
        spare = loss_rows.shape[2]
        parts.append(jnp.zeros((spare - len(parts), width), jnp.float32))
        tail = jnp.concatenate(parts).astype(bf16)
        for s in range(seq_count):
            loss_rows[0, s] = tail
        copies = [
            pltpu.make_async_copy(
                loss_rows.at[0], out_ref.at[i, :, rows : rows + spare, :], sems.at[seg_count + i]
            )
            for i in range(seg_count)
        ]
        for copy in copies:
            copy.start()
        grads = sums[...].astype(bf16).reshape(-1, width)
        for share_ref in share_refs:
            share_ref[2 * comp_rows :, :] = grads
        for i in range(seg_count):
            copy_out(i).wait()
        for copy in copies:
            copy.wait()


def head(starts, at, recv, conv_keys, conv_values):
    seg_count, seq_count, block, width = recv.shape
    rows = block * seg_count // (3 * seg_count + 2)
    share = rows // seg_count
    seg_rows = rows * seq_count
    comp_rows = seg_rows // RATE
    step = math.gcd(seg_rows, 256)
    bf16, f32 = jnp.bfloat16, jnp.float32
    shape = jax.ShapeDtypeStruct
    spare = 16
    share_shape = (2 * comp_rows + 2 * RATE * width, width)
    conv = pl.BlockSpec((1, RATE * width, width), lambda g, starts, at: (at[0], 0, 0))

    def body(starts_ref, at_ref, *refs):
        head_kernel((rows, seq_count, step), starts_ref, at_ref, *refs)

    return pl.pallas_call(
        body,
        out_shape=(
            shape((seg_count, seq_count, rows + spare, width), bf16),
            *[shape(share_shape, bf16)] * seg_count,
        ),
        grid_spec=pltpu.PrefetchScalarGridSpec(
            num_scalar_prefetch=2,
            grid=(seg_count,),
            in_specs=[
                pl.BlockSpec((1, seq_count, 3 * rows, width), lambda g, starts, at: (g, 0, 0, 0)),
                pl.BlockSpec(
                    (seg_count, seq_count, 2 * share, width),
                    lambda g, starts, at: (0, 0, 3 * rows // (2 * share), 0),
                ),
                conv,
                conv,
            ],
            out_specs=(
                pl.BlockSpec(memory_space=pl.ANY),
                *[pl.BlockSpec(share_shape, lambda g, starts, at: (0, 0))] * seg_count,
            ),
            scratch_shapes=[
                pltpu.VMEM((seg_count, seq_count, rows, width), bf16),
                pltpu.VMEM((1, seq_count, spare, width), bf16),
                pltpu.VMEM((2, comp_rows, width), bf16),
                pltpu.VMEM((seg_rows, width), bf16),
                pltpu.VMEM((seg_rows, 2 * width), bf16),
                pltpu.VMEM((comp_rows + seg_rows, width), bf16),
                pltpu.VMEM((comp_rows + seg_rows, 2 * width), bf16),
                pltpu.VMEM((seg_rows, width), f32),
                pltpu.VMEM((comp_rows, RATE * width), bf16),
                pltpu.VMEM((comp_rows, RATE * width), bf16),
                pltpu.VMEM((seg_rows, comp_rows), bf16),
                pltpu.VMEM((seg_rows, width), bf16),
                pltpu.VMEM((seg_rows, comp_rows), bf16),
                pltpu.VMEM((2, RATE * width, width), f32),
                pltpu.VMEM((1, width), f32),
                pltpu.SemaphoreType.DMA((2 * seg_count,)),
            ],
        ),
        compiler_params=on_vmem(28),
        cost_estimate=pl.CostEstimate(
            flops=20 * seg_count * seg_rows * seg_rows * width, bytes_accessed=2**23, transcendentals=0
        ),
        name="head",
    )(starts, at, recv, recv, conv_keys, conv_values)


def share_kernel(at_ref, *refs):
    shares, (comp_k_ref, comp_v_ref, grad_k_ref, grad_v_ref) = refs[:-4], refs[-4:]
    heads, taps, width = grad_k_ref.shape
    comp_rows = comp_k_ref.shape[0]
    for step, ref in enumerate(shares):
        head_at = lax.rem(at_ref[0] - step + heads, heads)
        columns = pl.ds(pl.multiple_of(head_at * width, width), width)
        comp_k_ref[:, columns] = ref[0:comp_rows, :]
        comp_v_ref[:, columns] = ref[comp_rows : 2 * comp_rows, :]
        grads = ref[2 * comp_rows :, :].astype(jnp.float32)
        grad_k_ref[head_at] = grads[0:taps]
        grad_v_ref[head_at] = grads[taps:]


def shared(at, shares, comp_rows, taps):
    heads = len(shares)
    width = shares[0].shape[1]
    arrived = [shares[0]]
    for step in range(1, heads):
        route = [(i, (i + step) % heads) for i in range(heads)]
        arrived.append(lax.ppermute(shares[step], "seg", route))
    comp = jax.ShapeDtypeStruct((comp_rows, heads * width), shares[0].dtype)
    grad = jax.ShapeDtypeStruct((heads, taps, width), jnp.float32)
    in_vmem = pl.BlockSpec(memory_space=pltpu.VMEM)
    return pl.pallas_call(
        share_kernel,
        out_shape=(comp, comp, grad, grad),
        in_specs=[pl.BlockSpec(memory_space=pltpu.SMEM), *[in_vmem] * heads],
        out_specs=(in_vmem,) * 4,
        compiler_params=on_vmem(12),
        name="shared",
    )(at, *arrived)


def head_on_device(
    queries, keys, values, prior_keys, prior_values, conv_keys, conv_values, doc_starts
):
    seq_count = lax.axis_size("seq")
    seg_count = lax.axis_size("seg")
    count = seg_count * seq_count
    rows = queries.shape[0]
    width = conv_keys.shape[2]
    at = lax.axis_index("seg").astype(jnp.int32).reshape(1)

    def exchanged(blocks):
        flat = blocks.reshape(count, -1, width)
        flat = lax.all_to_all(flat, BOTH, split_axis=0, concat_axis=0, tiled=True)
        return flat.reshape(blocks.shape)

    packed = pack(at, (queries, keys, values), (prior_keys, prior_values), seg_count, seq_count)
    attended, *shares = head(doc_starts, at, exchanged(packed), conv_keys, conv_values)
    attended, loss = unpack(exchanged(attended), rows, count * rows)
    comp_keys, comp_values, grad_k, grad_v = shared(
        at, shares, rows * seq_count // RATE, conv_keys.shape[1]
    )
    return (attended, comp_keys, comp_values, loss[0, 0], grad_k, grad_v)


def shifted_2(block, axis, distance):
    devices = range(lax.axis_size(axis))
    route = [(i - distance, i) for i in devices if i - distance in devices]
    return lax.ppermute(block, axis, route)


def pick_entry(small_table, wanted):
    return jnp.sum(jnp.where(jnp.arange(small_table.shape[0]) == wanted, small_table, 0))


def compress(source_rows, weight):
    head_count = weight.shape[0]
    head_width = weight.shape[2]
    windows = source_rows.reshape(source_rows.shape[0] // RATE, RATE, head_count, head_width)
    kernel = weight.reshape(head_count, RATE, head_width, head_width)
    merged = jnp.einsum("crhd,hrde->che", windows, kernel, preferred_element_type=jnp.float32)
    return merged.reshape(merged.shape[0], head_count * head_width).astype(jnp.bfloat16)


def on_device(queries, keys, values, prior_keys, prior_values, conv_keys, conv_values, doc_starts):
    seq_count = lax.axis_size("seq")
    seg_count = lax.axis_size("seg")
    group_index = lax.axis_index("seg")
    seg_rows = queries.shape[0] * seq_count
    head_count = conv_keys.shape[0]
    head_width = conv_keys.shape[2]
    comp_rows = seg_rows // RATE
    score_scale = 1.0 / math.sqrt(head_width)
    first_group = group_index == 0
    shifted = shifted_2(jnp.stack((keys, values)), "seg", 1)
    previous = jnp.where(first_group, jnp.stack((prior_keys, prior_values)), shifted)
    moved = (
        lax.all_to_all(queries, "seq", split_axis=1, concat_axis=0, tiled=True),
        lax.all_to_all(keys, "seq", split_axis=1, concat_axis=0, tiled=True),
        lax.all_to_all(values, "seq", split_axis=1, concat_axis=0, tiled=True),
        lax.all_to_all(previous[0], "seq", split_axis=1, concat_axis=0, tiled=True),
        lax.all_to_all(previous[1], "seq", split_axis=1, concat_axis=0, tiled=True),
    )
    query_heads = moved[0]
    key_heads = moved[1]
    value_heads = moved[2]
    fine_keys = moved[3]
    fine_values = moved[4]
    comp_keys = compress(fine_keys, conv_keys)
    comp_values = compress(fine_values, conv_values)
    memory = shifted_2(jnp.stack((comp_keys, comp_values)), "seg", 1)
    start_now = pick_entry(doc_starts, group_index)
    start_prev = jnp.where(group_index >= 1, pick_entry(doc_starts, group_index - 1), seg_rows)
    start_back = jnp.where(group_index >= 2, pick_entry(doc_starts, group_index - 2), seg_rows)
    lead_prev = jnp.where(start_prev < seg_rows, start_prev, 0)
    lead_back = jnp.where(start_back < seg_rows, start_back, 0)
    comp_open = (group_index >= 1) & (start_prev >= seg_rows)
    all_keys = jnp.concatenate((memory[0], fine_keys, key_heads), axis=0)
    all_values = jnp.concatenate((memory[1], fine_values, value_heads), axis=0)
    block_rows = math.gcd(seg_rows, 512)
    block_count = seg_rows // block_rows
    column = jnp.arange(comp_rows + 2 * seg_rows, dtype=jnp.int32)[None, :]
    comp_part = column < comp_rows
    fine_part = (column >= comp_rows) & (column < comp_rows + seg_rows)
    own_part = column >= comp_rows + seg_rows
    key_place = jnp.where(
        comp_part,
        RATE * column,
        jnp.where(fine_part, column - comp_rows, column - comp_rows - seg_rows),
    )

    def attend_block(flat_index):
        head_index = flat_index // block_count
        block_index = flat_index % block_count
        query_block = lax.dynamic_slice(
            query_heads,
            (block_index * block_rows, head_index * head_width),
            (block_rows, head_width),
        )
        key_block = lax.dynamic_slice_in_dim(all_keys, head_index * head_width, head_width, 1)
        value_block = lax.dynamic_slice_in_dim(all_values, head_index * head_width, head_width, 1)
        scores = (
            jnp.einsum("qd,kd->qk", query_block, key_block, preferred_element_type=jnp.float32)
            * score_scale
        )
        query_place = block_index * block_rows + jnp.arange(block_rows, dtype=jnp.int32)[:, None]
        before_doc = query_place < start_now
        seen_comp = comp_part & comp_open & before_doc & (key_place >= lead_back)
        seen_fine = fine_part & before_doc & (key_place >= lead_prev)
        seen_own = own_part & (key_place <= query_place) & ((key_place >= start_now) | before_doc)
        visible = seen_comp | seen_fine | seen_own
        row_top = jnp.max(jnp.where(visible, scores, -jnp.inf), axis=1, keepdims=True)
        weights = jnp.exp(jnp.where(visible, scores - row_top, -jnp.inf))
        row_total = jnp.sum(weights, axis=1, keepdims=True)
        mixed_rows = (
            jnp.dot(weights.astype(jnp.bfloat16), value_block, preferred_element_type=jnp.float32)
            / row_total
        )
        return mixed_rows.astype(jnp.bfloat16)

    pieces = lax.map(attend_block, jnp.arange(head_count * block_count, dtype=jnp.int32))
    attended_heads = (
        pieces.reshape(head_count, seg_rows, head_width)
        .transpose(1, 0, 2)
        .reshape(seg_rows, head_count * head_width)
    )
    attended = lax.all_to_all(attended_heads, "seq", split_axis=0, concat_axis=1, tiled=True)

    def recon_head(head_index):
        start_col = head_index * head_width
        query_full = lax.dynamic_slice_in_dim(query_heads, start_col, head_width, 1)
        fine_k = lax.dynamic_slice_in_dim(fine_keys, start_col, head_width, 1)
        fine_v = lax.dynamic_slice_in_dim(fine_values, start_col, head_width, 1)
        comp_k = lax.dynamic_slice_in_dim(comp_keys, start_col, head_width, 1)
        comp_v = lax.dynamic_slice_in_dim(comp_values, start_col, head_width, 1)

        def recon_step(running, block_index):
            loss_sum, value_acc, key_acc = running
            query_block = lax.dynamic_slice_in_dim(
                query_full, block_index * block_rows, block_rows, 0
            )
            fine_scores = (
                jnp.einsum("qd,kd->qk", query_block, fine_k, preferred_element_type=jnp.float32)
                * score_scale
            )
            fine_exp = jnp.exp(fine_scores - jnp.max(fine_scores, axis=1, keepdims=True))
            fine_total = jnp.sum(fine_exp, axis=1, keepdims=True)
            recon_fine = (
                jnp.dot(fine_exp.astype(jnp.bfloat16), fine_v, preferred_element_type=jnp.float32)
                / fine_total
            )
            comp_scores = (
                jnp.einsum("qd,kd->qk", query_block, comp_k, preferred_element_type=jnp.float32)
                * score_scale
            )
            comp_exp = jnp.exp(comp_scores - jnp.max(comp_scores, axis=1, keepdims=True))
            comp_total = jnp.sum(comp_exp, axis=1, keepdims=True)
            comp_weights = comp_exp.astype(jnp.bfloat16)
            recon_comp = (
                jnp.dot(comp_weights, comp_v, preferred_element_type=jnp.float32) / comp_total
            )
            differ = recon_fine - recon_comp
            out_grad = (-2.0 * differ / comp_total).astype(jnp.bfloat16)
            value_acc = value_acc + jnp.einsum(
                "qc,qd->cd", comp_weights, out_grad, preferred_element_type=jnp.float32
            )
            inner_grad = jnp.einsum(
                "qd,cd->qc", out_grad, comp_v, preferred_element_type=jnp.float32
            )
            row_offset = jnp.sum(out_grad.astype(jnp.float32) * recon_comp, axis=1, keepdims=True)
            score_grad = (comp_exp * (inner_grad - row_offset)).astype(jnp.bfloat16)
            key_acc = key_acc + jnp.einsum(
                "qc,qd->cd", score_grad, query_block, preferred_element_type=jnp.float32
            )
            return ((loss_sum + jnp.sum(differ * differ), value_acc, key_acc), None)

        zero_rows = jnp.zeros((comp_rows, head_width), jnp.float32)
        start_state = (jnp.zeros((), jnp.float32), zero_rows, zero_rows)
        (loss_sum, value_acc, key_acc), unused = lax.scan(
            recon_step, start_state, jnp.arange(block_count, dtype=jnp.int32)
        )
        key_grad = (key_acc * score_scale).astype(jnp.bfloat16)
        value_grad = value_acc.astype(jnp.bfloat16)
        windows_k = fine_k.reshape(comp_rows, RATE * head_width)
        windows_v = fine_v.reshape(comp_rows, RATE * head_width)
        grad_k = jnp.einsum("cw,cd->wd", windows_k, key_grad, preferred_element_type=jnp.float32)
        grad_v = jnp.einsum("cw,cd->wd", windows_v, value_grad, preferred_element_type=jnp.float32)
        return (loss_sum, grad_k, grad_v)

    losses, grad_k, grad_v = lax.map(recon_head, jnp.arange(head_count, dtype=jnp.int32))
    grad_k, grad_v = (
        lax.psum(grad_k.astype(jnp.bfloat16), "seg").astype(jnp.float32),
        lax.psum(grad_v.astype(jnp.bfloat16), "seg").astype(jnp.float32),
    )
    total_loss = lax.psum(jnp.sum(losses), ("seg", "seq"))
    recon_loss = total_loss / (seg_count * seg_rows)
    return (attended, comp_keys, comp_values, recon_loss, grad_k, grad_v)


def solution(mesh):
    def body(*arrays):
        heads, width = arrays[5].shape[0], arrays[5].shape[2]
        rows = arrays[0].shape[0]
        by_head = heads == mesh.shape["seg"] and width % 128 == 0
        by_head = by_head and all(n & (n - 1) == 0 for n in mesh.shape.values())
        by_head = by_head and heads % 2 == 0 and rows % (16 * heads) == 0 and 256 % rows == 0
        return (head_on_device if by_head else on_device)(*arrays)

    return jax.shard_map(
        body,
        mesh=mesh,
        in_specs=(
            P(("seg", "seq"), None),
            P(("seg", "seq"), None),
            P(("seg", "seq"), None),
            P("seq", None),
            P("seq", None),
            P("seq", None, None),
            P("seq", None, None),
            P(),
        ),
        out_specs=(
            P(("seg", "seq"), None),
            P("seg", "seq"),
            P("seg", "seq"),
            P(),
            P("seq", None, None),
            P("seq", None, None),
        ),
        check_vma=False,
    )
```

```python
import functools
import math

import jax
import jax.numpy as jnp
from jax import lax
from jax.experimental import pallas as pl
from jax.experimental.pallas import tpu as pltpu
from jax.sharding import PartitionSpec as P

RATE = 4
HIDDEN = -1e30
STEP = 512
AHEAD = 2
BOTH = ("seq", "seg")


def on_vmem(limit_mib=60):
    return pltpu.CompilerParams(vmem_limit_bytes=limit_mib * 2**20)


def pack_kernel(at_ref, *refs):
    del at_ref
    out_ref = refs[-1]
    seq_count, seg_count, _, width = out_ref.shape
    for s in range(seq_count):
        for r in range(seg_count):
            column = (s * seg_count + r) * width
            row = 0
            for ref in refs[:-1]:
                rows = ref.shape[0]
                out_ref[s, r, row : row + rows, :] = ref[:, column : column + width]
                row += rows


def pack(at, arrays, prior_arrays, seg_count, seq_count):
    rows, columns = arrays[0].shape
    width = columns // (seg_count * seq_count)
    share = rows // seg_count
    block = len(arrays) * rows + len(prior_arrays) * share
    steps = 2
    wide = columns // steps
    return pl.pallas_call(
        pack_kernel,
        out_shape=jax.ShapeDtypeStruct((seq_count, seg_count, block, width), arrays[0].dtype),
        grid_spec=pltpu.PrefetchScalarGridSpec(
            num_scalar_prefetch=1,
            grid=(steps,),
            in_specs=[
                *[pl.BlockSpec((rows, wide), lambda s, at: (0, s))] * len(arrays),
                *[pl.BlockSpec((share, wide), lambda s, at: (at[0], s))] * len(prior_arrays),
            ],
            out_specs=pl.BlockSpec(
                (seq_count // steps, seg_count, block, width), lambda s, at: (s, 0, 0, 0)
            ),
        ),
        compiler_params=on_vmem(),
        name="pack",
    )(at, *arrays, *prior_arrays)


def unpack_kernel(positions, in_ref, out_ref, loss_ref, rows_ref, tails, sems):
    seq_count, seg_count, _, width = in_ref.shape
    rows = rows_ref.shape[0]
    copies = []
    for s in range(seq_count):
        for r in range(seg_count):
            at = s * seg_count + r
            columns = slice(at * width, (at + 1) * width)
            from_ref = in_ref.at[s, r, 0:rows, :]
            copies.append(pltpu.make_async_copy(from_ref, rows_ref.at[:, columns], sems.at[at]))
            copies[-1].start()
    spare = tails.shape[2]
    tail = pltpu.make_async_copy(
        in_ref.at[:, :, rows : rows + spare, :], tails, sems.at[seg_count * seq_count]
    )
    tail.start()
    for copy in copies:
        copy.wait()
    copy = pltpu.make_async_copy(rows_ref, out_ref, sems.at[seg_count * seq_count + 1])
    copy.start()
    tail.wait()
    parts = tails[...].reshape(-1, width).astype(jnp.float32)
    total = jnp.sum(jnp.sum(parts, axis=0, keepdims=True), axis=1, keepdims=True)
    loss_ref[...] = total / positions
    copy.wait()


def unpack(blocks, rows, positions):
    seq_count, seg_count, _, width = blocks.shape
    spare = blocks.shape[2] - rows
    shape = (rows, seg_count * seq_count * width)
    return pl.pallas_call(
        functools.partial(unpack_kernel, positions),
        out_shape=(
            jax.ShapeDtypeStruct(shape, blocks.dtype),
            jax.ShapeDtypeStruct((1, 1), jnp.float32),
        ),
        in_specs=[pl.BlockSpec(memory_space=pl.ANY)],
        out_specs=(
            pl.BlockSpec(memory_space=pl.ANY),
            pl.BlockSpec(memory_space=pltpu.VMEM),
        ),
        scratch_shapes=[
            pltpu.VMEM(shape, blocks.dtype),
            pltpu.VMEM((seq_count, seg_count, spare, width), blocks.dtype),
            pltpu.SemaphoreType.DMA((seg_count * seq_count + 2,)),
        ],
        compiler_params=on_vmem(8),
        name="unpack",
    )(blocks)


def matmul_t(a, b):
    return lax.dot_general(a, b, (((1,), (1,)), ((), ())), preferred_element_type=jnp.float32)


def t_matmul(a, b):
    return lax.dot_general(a, b, (((0,), (0,)), ((), ())), preferred_element_type=jnp.float32)


def matmul(a, b):
    return jnp.dot(a, b, preferred_element_type=jnp.float32)


def softmax_part(scores, rate):
    top = jnp.max(scores, axis=1, keepdims=True)
    return top, jnp.exp2((scores - top) * rate)


def merge_taps(fine, conv, comp, win, rows_f32):
    comp_rows, width = comp.shape
    rows_f32[...] = fine[:, 0:width].astype(jnp.float32)
    for r in range(RATE):
        taps = rows_f32[pl.ds(r, comp_rows, stride=RATE), :]
        win[:, r * width : (r + 1) * width] = taps.astype(jnp.bfloat16)
    comp[...] = matmul(win[...], conv[0]).astype(jnp.bfloat16)


def doc_bounds(starts_ref, g, seg_rows, comp_rows):
    def start_of(i):
        return jnp.where(i >= 0, starts_ref[jnp.maximum(i, 0)], seg_rows)

    b0, b1, b2 = start_of(g), start_of(g - 1), start_of(g - 2)
    s1 = jnp.where(b1 < seg_rows, b1, 0)
    s2 = jnp.where(b2 < seg_rows, b2, 0)
    memory_from = jnp.where((g >= 1) & (b1 >= seg_rows), s2, RATE * comp_rows)
    return b0, s1, memory_from


def memory_scores(scores, p0, b0, memory_from):
    place_q = p0 + lax.broadcasted_iota(jnp.int32, scores.shape, 0)
    place_k = RATE * lax.broadcasted_iota(jnp.int32, scores.shape, 1)
    return jnp.where((place_q < b0) & (place_k >= memory_from), scores, HIDDEN)


def own_scores(scores, p0, b0):
    place_q = p0 + lax.broadcasted_iota(jnp.int32, scores.shape, 0)
    place_k = lax.broadcasted_iota(jnp.int32, scores.shape, 1)
    seen = (place_k <= place_q) & ((place_k >= b0) | (place_q < b0))
    return jnp.where(seen, scores, HIDDEN)


def before_doc(step, p0, b0):
    return p0 + lax.broadcasted_iota(jnp.int32, (step, 1), 0) < b0


def head_kernel(
    dims, starts_ref, at_ref, recv_ref, prior_ref, conv_k_ref, conv_v_ref,
    out_ref, grad_ref, *rest,
):
    rows, seq_count, step = dims
    share_refs, rest = rest[: prior_ref.shape[1]], rest[prior_ref.shape[1] :]
    (
        out_rows, loss_rows, comp_ref, fine_k, fine_v, cat_k, cat_v, rows_f32,
        win_k, win_v, sums, losses, sems,
    ) = rest
    g = pl.program_id(0)
    seg_rows = rows * seq_count
    comp_rows = seg_rows // RATE
    _, seg_count, both_shares, width = prior_ref.shape
    share = both_shares // 2
    scale = 1.0 / math.sqrt(width)
    rate = math.log2(math.e) * scale
    bf16 = jnp.bfloat16

    @pl.when(g == 0)
    def _():
        cat_k[0:comp_rows, :] = jnp.zeros((comp_rows, width), bf16)
        cat_v[0:comp_rows, 0:width] = jnp.zeros((comp_rows, width), bf16)
        cat_v[:, width:] = jnp.ones((comp_rows + seg_rows, width), bf16)
        fine_v[:, width:] = jnp.ones((seg_rows, width), bf16)
        sums[...] = jnp.zeros_like(sums)
        losses[...] = jnp.zeros_like(losses)
        for s in range(seq_count):
            for i in range(seg_count):
                at = s * rows + i * share
                fine_k[at : at + share, :] = prior_ref[s, i, 0:share, :]
                fine_v[at : at + share, 0:width] = prior_ref[s, i, share:, :]

    @pl.when(g > 0)
    def _():
        fine_k[...] = cat_k[comp_rows:, :]
        fine_v[:, 0:width] = cat_v[comp_rows:, 0:width]

    cat_k[comp_rows:, :] = recv_ref[:, 0, rows : 2 * rows, :].reshape(seg_rows, width)
    cat_v[comp_rows:, 0:width] = recv_ref[:, 0, 2 * rows : 3 * rows, :].reshape(seg_rows, width)
    merge_taps(fine_k, conv_k_ref, comp_ref.at[0], win_k, rows_f32)
    merge_taps(fine_v, conv_v_ref, comp_ref.at[1], win_v, rows_f32)
    comp_k, comp_v = comp_ref[0], comp_ref[1]
    for i, share_ref in enumerate(share_refs):

        @pl.when(lax.rem(g - at_ref[0] + seg_count, seg_count) == i)
        def _():
            share_ref[...] = comp_ref[...]

    b0, s1, memory_from = doc_bounds(starts_ref, g, seg_rows, comp_rows)

    def queries(p0):
        return recv_ref[p0 // rows : (p0 + step) // rows, 0, 0:rows, :].reshape(step, width)

    def weighted(weights, values_and_ones):
        mix = matmul(weights.astype(bf16), values_and_ones)
        return mix[:, 0:width], mix[:, width:]

    def attend(fine_from_s1):
        fine, recon = {}, {}
        value_rows, key_rows = [], []

        def fine_scores(p0):
            return matmul_t(queries(p0), fine_k[...])

        def fine_part(p0, scores):
            top, weights = softmax_part(scores, rate)
            mix, total = weighted(weights, fine_v[...])
            recon[p0] = mix / total
            if fine_from_s1:
                place = lax.broadcasted_iota(jnp.int32, scores.shape, 1)
                top, weights = softmax_part(jnp.where(place >= s1, scores, HIDDEN), rate)
                mix, total = weighted(weights, fine_v[...])
            fine[p0] = top, mix, total

        def comp_scores(p0):
            return matmul_t(queries(p0), comp_k)

        def comp_part(p0, scores):
            _, comp_exp = softmax_part(scores, rate)
            total = jnp.sum(comp_exp, axis=1, keepdims=True)
            weights = comp_exp.astype(bf16)
            recon_comp = matmul(weights, comp_v) / total
            differ = recon.pop(p0) - recon_comp
            losses[...] += jnp.sum(differ * differ, axis=0, keepdims=True)
            out_grad = (-2.0 * differ / total).astype(bf16)
            inner = matmul_t(out_grad, comp_v)
            offset = jnp.sum(out_grad.astype(jnp.float32) * recon_comp, axis=1, keepdims=True)
            score_grad = (comp_exp * (inner - offset)).astype(bf16)
            value_rows.append(t_matmul(weights, out_grad))
            key_rows.append(t_matmul(score_grad, queries(p0)))

        def cat_scores(p0):
            scores = matmul_t(queries(p0), cat_k[0 : comp_rows + p0 + step, :])
            memory = memory_scores(scores[:, 0:comp_rows], p0, b0, memory_from)
            return jnp.concatenate((memory, own_scores(scores[:, comp_rows:], p0, b0)), axis=1)

        def cat_part(p0, scores):
            top, weights = softmax_part(scores, rate)
            mix, total = weighted(weights, cat_v[0 : comp_rows + p0 + step, :])
            fine_top, fine_mix, fine_total = fine.pop(p0)
            seen = before_doc(step, p0, b0)
            both = jnp.where(seen, jnp.maximum(top, fine_top), top)
            fine_share = jnp.where(seen, jnp.exp2((fine_top - both) * rate), 0.0)
            cat_share = jnp.exp2((top - both) * rate)
            mix = mix * cat_share + fine_mix * fine_share
            total = total * cat_share + fine_total * fine_share
            here = slice(p0 // rows, (p0 + step) // rows)
            out_rows[g, here] = (mix / total).astype(bf16).reshape(step // rows, rows, width)

        parts = [
            (p0, *part)
            for p0 in range(0, seg_rows, step)
            for part in ((fine_scores, fine_part), (cat_scores, cat_part), (comp_scores, comp_part))
        ]
        asked = [ask(p0) for p0, ask, _ in parts[:AHEAD]]
        for i, (p0, _, finish) in enumerate(parts):
            if i + AHEAD < len(parts):
                asked.append(parts[i + AHEAD][1](parts[i + AHEAD][0]))
            finish(p0, asked.pop(0))
        sums[0] += t_matmul(win_k[...], (sum(key_rows) * scale).astype(bf16))
        sums[1] += t_matmul(win_v[...], sum(value_rows).astype(bf16))

    @pl.when(s1 <= 0)
    def _():
        attend(False)

    @pl.when(s1 > 0)
    def _():
        attend(True)

    def copy_out(i):
        return pltpu.make_async_copy(out_rows.at[i], out_ref.at[:, i, 0:rows, :], sems.at[i])

    copy_out(g).start()
    cat_k[0:comp_rows, :] = comp_k
    cat_v[0:comp_rows, 0:width] = comp_v
    @pl.when(g == seg_count - 1)
    def _():
        left = losses[...]
        parts = []
        for _ in range(3):
            parts.append(left.astype(bf16).astype(jnp.float32))
            left = left - parts[-1]
        spare = loss_rows.shape[2]
        parts.append(jnp.zeros((spare - len(parts), width), jnp.float32))
        tail = jnp.concatenate(parts).astype(bf16)
        for s in range(seq_count):
            loss_rows[0, s] = tail
        copies = [
            pltpu.make_async_copy(
                loss_rows.at[0], out_ref.at[:, i, rows : rows + spare, :], sems.at[seg_count + i]
            )
            for i in range(seg_count)
        ]
        for copy in copies:
            copy.start()
        grad_ref[...] = sums[...].astype(bf16)
        for i in range(seg_count):
            copy_out(i).wait()
        for copy in copies:
            copy.wait()


def head(starts, at, recv, conv_keys, conv_values):
    seq_count, seg_count, block, width = recv.shape
    rows = block * seg_count // (3 * seg_count + 2)
    share = rows // seg_count
    seg_rows = rows * seq_count
    comp_rows = seg_rows // RATE
    step = math.gcd(seg_rows, STEP)
    bf16, f32 = jnp.bfloat16, jnp.float32
    shape = jax.ShapeDtypeStruct
    spare = 8
    comp_shape = (2, comp_rows, width)
    grad_shape = (2, RATE * width, width)
    conv = pl.BlockSpec((1, RATE * width, width), lambda g, starts, at: (at[0], 0, 0))

    def body(starts_ref, at_ref, *refs):
        head_kernel((rows, seq_count, step), starts_ref, at_ref, *refs)

    return pl.pallas_call(
        body,
        out_shape=(
            shape((seq_count, seg_count, rows + spare, width), bf16),
            shape(grad_shape, bf16),
            *[shape(comp_shape, bf16)] * seg_count,
        ),
        grid_spec=pltpu.PrefetchScalarGridSpec(
            num_scalar_prefetch=2,
            grid=(seg_count,),
            in_specs=[
                pl.BlockSpec((seq_count, 1, 3 * rows, width), lambda g, starts, at: (0, g, 0, 0)),
                pl.BlockSpec(
                    (seq_count, seg_count, 2 * share, width),
                    lambda g, starts, at: (0, 0, 3 * rows // (2 * share), 0),
                ),
                conv,
                conv,
            ],
            out_specs=(
                pl.BlockSpec(memory_space=pl.ANY),
                pl.BlockSpec(grad_shape, lambda g, starts, at: (0, 0, 0)),
                *[pl.BlockSpec(comp_shape, lambda g, starts, at: (0, 0, 0))] * seg_count,
            ),
            scratch_shapes=[
                pltpu.VMEM((seg_count, seq_count, rows, width), bf16),
                pltpu.VMEM((1, seq_count, spare, width), bf16),
                pltpu.VMEM((2, comp_rows, width), bf16),
                pltpu.VMEM((seg_rows, width), bf16),
                pltpu.VMEM((seg_rows, 2 * width), bf16),
                pltpu.VMEM((comp_rows + seg_rows, width), bf16),
                pltpu.VMEM((comp_rows + seg_rows, 2 * width), bf16),
                pltpu.VMEM((seg_rows, width), f32),
                pltpu.VMEM((comp_rows, RATE * width), bf16),
                pltpu.VMEM((comp_rows, RATE * width), bf16),
                pltpu.VMEM((2, RATE * width, width), f32),
                pltpu.VMEM((1, width), f32),
                pltpu.SemaphoreType.DMA((2 * seg_count,)),
            ],
        ),
        compiler_params=on_vmem(28),
        cost_estimate=pl.CostEstimate(
            flops=20 * seg_count * seg_rows * seg_rows * width, bytes_accessed=2**23, transcendentals=0
        ),
        name="head",
    )(starts, at, recv, recv, conv_keys, conv_values)


def share_kernel(at_ref, *refs):
    arrived, (comp_k_ref, comp_v_ref, grad_k_ref, grad_v_ref) = refs[:-4], refs[-4:]
    heads, _, width = grad_k_ref.shape
    for step, ref in enumerate(arrived[:heads]):
        head_at = lax.rem(at_ref[0] - step + heads, heads)
        columns = pl.ds(pl.multiple_of(head_at * width, width), width)
        comp_k_ref[:, columns] = ref[0]
        comp_v_ref[:, columns] = ref[1]
    for step, ref in enumerate(arrived[heads:]):
        grads = ref[...].astype(jnp.float32)
        grad_k_ref[at_ref[0] ^ step] = grads[0]
        grad_v_ref[at_ref[0] ^ step] = grads[1]


def shared(at, comps, grads):
    heads = len(comps)
    comp_rows, width = comps[0].shape[1:]
    arrived = [comps[0]]
    for step in range(1, heads):
        route = [(i, (i + step) % heads) for i in range(heads)]
        arrived.append(lax.ppermute(comps[step], "seg", route))
    held = {0: grads}
    bit = heads // 2
    while bit:
        route = [(i, i ^ bit) for i in range(heads)]
        held |= {k ^ bit: lax.ppermute(x, "seg", route) for k, x in held.items()}
        bit //= 2
    arrived += [held[k] for k in range(heads)]
    comp = jax.ShapeDtypeStruct((comp_rows, heads * width), grads.dtype)
    grad = jax.ShapeDtypeStruct((heads, *grads.shape[1:]), jnp.float32)
    in_vmem = pl.BlockSpec(memory_space=pltpu.VMEM)
    return pl.pallas_call(
        share_kernel,
        out_shape=(comp, comp, grad, grad),
        in_specs=[pl.BlockSpec(memory_space=pltpu.SMEM), *[in_vmem] * len(arrived)],
        out_specs=(in_vmem,) * 4,
        compiler_params=on_vmem(12),
        name="shared",
    )(at, *arrived)


def head_on_device(
    queries, keys, values, prior_keys, prior_values, conv_keys, conv_values, doc_starts
):
    seq_count = lax.axis_size("seq")
    seg_count = lax.axis_size("seg")
    count = seg_count * seq_count
    rows = queries.shape[0]
    width = conv_keys.shape[2]
    at = lax.axis_index("seg").astype(jnp.int32).reshape(1)

    def exchanged(blocks):
        flat = blocks.reshape(count, -1, width)
        flat = lax.all_to_all(flat, BOTH, split_axis=0, concat_axis=0, tiled=True)
        return flat.reshape(blocks.shape)

    packed = pack(at, (queries, keys, values), (prior_keys, prior_values), seg_count, seq_count)
    attended, grads, *comps = head(doc_starts, at, exchanged(packed), conv_keys, conv_values)
    attended, loss = unpack(exchanged(attended), rows, count * rows)
    comp_keys, comp_values, grad_k, grad_v = shared(at, comps, grads)
    return (attended, comp_keys, comp_values, loss[0, 0], grad_k, grad_v)


def shifted_2(block, axis, distance):
    devices = range(lax.axis_size(axis))
    route = [(i - distance, i) for i in devices if i - distance in devices]
    return lax.ppermute(block, axis, route)


def pick_entry(small_table, wanted):
    return jnp.sum(jnp.where(jnp.arange(small_table.shape[0]) == wanted, small_table, 0))


def compress(source_rows, weight):
    head_count = weight.shape[0]
    head_width = weight.shape[2]
    windows = source_rows.reshape(source_rows.shape[0] // RATE, RATE, head_count, head_width)
    kernel = weight.reshape(head_count, RATE, head_width, head_width)
    merged = jnp.einsum("crhd,hrde->che", windows, kernel, preferred_element_type=jnp.float32)
    return merged.reshape(merged.shape[0], head_count * head_width).astype(jnp.bfloat16)


def on_device(queries, keys, values, prior_keys, prior_values, conv_keys, conv_values, doc_starts):
    seq_count = lax.axis_size("seq")
    seg_count = lax.axis_size("seg")
    group_index = lax.axis_index("seg")
    seg_rows = queries.shape[0] * seq_count
    head_count = conv_keys.shape[0]
    head_width = conv_keys.shape[2]
    comp_rows = seg_rows // RATE
    score_scale = 1.0 / math.sqrt(head_width)
    first_group = group_index == 0
    shifted = shifted_2(jnp.stack((keys, values)), "seg", 1)
    previous = jnp.where(first_group, jnp.stack((prior_keys, prior_values)), shifted)
    moved = (
        lax.all_to_all(queries, "seq", split_axis=1, concat_axis=0, tiled=True),
        lax.all_to_all(keys, "seq", split_axis=1, concat_axis=0, tiled=True),
        lax.all_to_all(values, "seq", split_axis=1, concat_axis=0, tiled=True),
        lax.all_to_all(previous[0], "seq", split_axis=1, concat_axis=0, tiled=True),
        lax.all_to_all(previous[1], "seq", split_axis=1, concat_axis=0, tiled=True),
    )
    query_heads = moved[0]
    key_heads = moved[1]
    value_heads = moved[2]
    fine_keys = moved[3]
    fine_values = moved[4]
    comp_keys = compress(fine_keys, conv_keys)
    comp_values = compress(fine_values, conv_values)
    memory = shifted_2(jnp.stack((comp_keys, comp_values)), "seg", 1)
    start_now = pick_entry(doc_starts, group_index)
    start_prev = jnp.where(group_index >= 1, pick_entry(doc_starts, group_index - 1), seg_rows)
    start_back = jnp.where(group_index >= 2, pick_entry(doc_starts, group_index - 2), seg_rows)
    lead_prev = jnp.where(start_prev < seg_rows, start_prev, 0)
    lead_back = jnp.where(start_back < seg_rows, start_back, 0)
    comp_open = (group_index >= 1) & (start_prev >= seg_rows)
    all_keys = jnp.concatenate((memory[0], fine_keys, key_heads), axis=0)
    all_values = jnp.concatenate((memory[1], fine_values, value_heads), axis=0)
    block_rows = math.gcd(seg_rows, 512)
    block_count = seg_rows // block_rows
    column = jnp.arange(comp_rows + 2 * seg_rows, dtype=jnp.int32)[None, :]
    comp_part = column < comp_rows
    fine_part = (column >= comp_rows) & (column < comp_rows + seg_rows)
    own_part = column >= comp_rows + seg_rows
    key_place = jnp.where(
        comp_part,
        RATE * column,
        jnp.where(fine_part, column - comp_rows, column - comp_rows - seg_rows),
    )

    def attend_block(flat_index):
        head_index = flat_index // block_count
        block_index = flat_index % block_count
        query_block = lax.dynamic_slice(
            query_heads,
            (block_index * block_rows, head_index * head_width),
            (block_rows, head_width),
        )
        key_block = lax.dynamic_slice_in_dim(all_keys, head_index * head_width, head_width, 1)
        value_block = lax.dynamic_slice_in_dim(all_values, head_index * head_width, head_width, 1)
        scores = (
            jnp.einsum("qd,kd->qk", query_block, key_block, preferred_element_type=jnp.float32)
            * score_scale
        )
        query_place = block_index * block_rows + jnp.arange(block_rows, dtype=jnp.int32)[:, None]
        before_doc = query_place < start_now
        seen_comp = comp_part & comp_open & before_doc & (key_place >= lead_back)
        seen_fine = fine_part & before_doc & (key_place >= lead_prev)
        seen_own = own_part & (key_place <= query_place) & ((key_place >= start_now) | before_doc)
        visible = seen_comp | seen_fine | seen_own
        row_top = jnp.max(jnp.where(visible, scores, -jnp.inf), axis=1, keepdims=True)
        weights = jnp.exp(jnp.where(visible, scores - row_top, -jnp.inf))
        row_total = jnp.sum(weights, axis=1, keepdims=True)
        mixed_rows = (
            jnp.dot(weights.astype(jnp.bfloat16), value_block, preferred_element_type=jnp.float32)
            / row_total
        )
        return mixed_rows.astype(jnp.bfloat16)

    pieces = lax.map(attend_block, jnp.arange(head_count * block_count, dtype=jnp.int32))
    attended_heads = (
        pieces.reshape(head_count, seg_rows, head_width)
        .transpose(1, 0, 2)
        .reshape(seg_rows, head_count * head_width)
    )
    attended = lax.all_to_all(attended_heads, "seq", split_axis=0, concat_axis=1, tiled=True)

    def recon_head(head_index):
        start_col = head_index * head_width
        query_full = lax.dynamic_slice_in_dim(query_heads, start_col, head_width, 1)
        fine_k = lax.dynamic_slice_in_dim(fine_keys, start_col, head_width, 1)
        fine_v = lax.dynamic_slice_in_dim(fine_values, start_col, head_width, 1)
        comp_k = lax.dynamic_slice_in_dim(comp_keys, start_col, head_width, 1)
        comp_v = lax.dynamic_slice_in_dim(comp_values, start_col, head_width, 1)

        def recon_step(running, block_index):
            loss_sum, value_acc, key_acc = running
            query_block = lax.dynamic_slice_in_dim(
                query_full, block_index * block_rows, block_rows, 0
            )
            fine_scores = (
                jnp.einsum("qd,kd->qk", query_block, fine_k, preferred_element_type=jnp.float32)
                * score_scale
            )
            fine_exp = jnp.exp(fine_scores - jnp.max(fine_scores, axis=1, keepdims=True))
            fine_total = jnp.sum(fine_exp, axis=1, keepdims=True)
            recon_fine = (
                jnp.dot(fine_exp.astype(jnp.bfloat16), fine_v, preferred_element_type=jnp.float32)
                / fine_total
            )
            comp_scores = (
                jnp.einsum("qd,kd->qk", query_block, comp_k, preferred_element_type=jnp.float32)
                * score_scale
            )
            comp_exp = jnp.exp(comp_scores - jnp.max(comp_scores, axis=1, keepdims=True))
            comp_total = jnp.sum(comp_exp, axis=1, keepdims=True)
            comp_weights = comp_exp.astype(jnp.bfloat16)
            recon_comp = (
                jnp.dot(comp_weights, comp_v, preferred_element_type=jnp.float32) / comp_total
            )
            differ = recon_fine - recon_comp
            out_grad = (-2.0 * differ / comp_total).astype(jnp.bfloat16)
            value_acc = value_acc + jnp.einsum(
                "qc,qd->cd", comp_weights, out_grad, preferred_element_type=jnp.float32
            )
            inner_grad = jnp.einsum(
                "qd,cd->qc", out_grad, comp_v, preferred_element_type=jnp.float32
            )
            row_offset = jnp.sum(out_grad.astype(jnp.float32) * recon_comp, axis=1, keepdims=True)
            score_grad = (comp_exp * (inner_grad - row_offset)).astype(jnp.bfloat16)
            key_acc = key_acc + jnp.einsum(
                "qc,qd->cd", score_grad, query_block, preferred_element_type=jnp.float32
            )
            return ((loss_sum + jnp.sum(differ * differ), value_acc, key_acc), None)

        zero_rows = jnp.zeros((comp_rows, head_width), jnp.float32)
        start_state = (jnp.zeros((), jnp.float32), zero_rows, zero_rows)
        (loss_sum, value_acc, key_acc), unused = lax.scan(
            recon_step, start_state, jnp.arange(block_count, dtype=jnp.int32)
        )
        key_grad = (key_acc * score_scale).astype(jnp.bfloat16)
        value_grad = value_acc.astype(jnp.bfloat16)
        windows_k = fine_k.reshape(comp_rows, RATE * head_width)
        windows_v = fine_v.reshape(comp_rows, RATE * head_width)
        grad_k = jnp.einsum("cw,cd->wd", windows_k, key_grad, preferred_element_type=jnp.float32)
        grad_v = jnp.einsum("cw,cd->wd", windows_v, value_grad, preferred_element_type=jnp.float32)
        return (loss_sum, grad_k, grad_v)

    losses, grad_k, grad_v = lax.map(recon_head, jnp.arange(head_count, dtype=jnp.int32))
    grad_k, grad_v = (
        lax.psum(grad_k.astype(jnp.bfloat16), "seg").astype(jnp.float32),
        lax.psum(grad_v.astype(jnp.bfloat16), "seg").astype(jnp.float32),
    )
    total_loss = lax.psum(jnp.sum(losses), ("seg", "seq"))
    recon_loss = total_loss / (seg_count * seg_rows)
    return (attended, comp_keys, comp_values, recon_loss, grad_k, grad_v)


def solution(mesh):
    def body(*arrays):
        heads, width = arrays[5].shape[0], arrays[5].shape[2]
        rows = arrays[0].shape[0]
        by_head = heads == mesh.shape["seg"] and width % 128 == 0
        by_head = by_head and all(n & (n - 1) == 0 for n in mesh.shape.values())
        by_head = by_head and heads % 2 == 0 and rows % (16 * heads) == 0 and 256 % rows == 0
        return (head_on_device if by_head else on_device)(*arrays)

    return jax.shard_map(
        body,
        mesh=mesh,
        in_specs=(
            P(("seg", "seq"), None),
            P(("seg", "seq"), None),
            P(("seg", "seq"), None),
            P("seq", None),
            P("seq", None),
            P("seq", None, None),
            P("seq", None, None),
            P(),
        ),
        out_specs=(
            P(("seg", "seq"), None),
            P("seg", "seq"),
            P("seg", "seq"),
            P(),
            P("seq", None, None),
            P("seq", None, None),
        ),
        check_vma=False,
    )
```

```python
import functools
import math

import jax
import jax.numpy as jnp
from jax import lax
from jax.experimental import pallas as pl
from jax.experimental.pallas import tpu as pltpu
from jax.sharding import PartitionSpec as P

RATE = 4
HIDDEN = -1e30
STEP = 512
AHEAD = 2
BOTH = ("seq", "seg")


def on_vmem(limit_mib=60):
    return pltpu.CompilerParams(vmem_limit_bytes=limit_mib * 2**20)


def pack_kernel(at_ref, *refs):
    del at_ref
    out_ref = refs[-1]
    seq_count, seg_count, _, width = out_ref.shape
    for s in range(seq_count):
        for r in range(seg_count):
            column = (s * seg_count + r) * width
            row = 0
            for ref in refs[:-1]:
                rows = ref.shape[0]
                out_ref[s, r, row : row + rows, :] = ref[:, column : column + width]
                row += rows


def pack(at, arrays, prior_arrays, seg_count, seq_count):
    rows, columns = arrays[0].shape
    width = columns // (seg_count * seq_count)
    share = rows // seg_count
    block = len(arrays) * rows + len(prior_arrays) * share
    steps = 2
    wide = columns // steps
    return pl.pallas_call(
        pack_kernel,
        out_shape=jax.ShapeDtypeStruct((seq_count, seg_count, block, width), arrays[0].dtype),
        grid_spec=pltpu.PrefetchScalarGridSpec(
            num_scalar_prefetch=1,
            grid=(steps,),
            in_specs=[
                *[pl.BlockSpec((rows, wide), lambda s, at: (0, s))] * len(arrays),
                *[pl.BlockSpec((share, wide), lambda s, at: (at[0], s))] * len(prior_arrays),
            ],
            out_specs=pl.BlockSpec(
                (seq_count // steps, seg_count, block, width), lambda s, at: (s, 0, 0, 0)
            ),
        ),
        compiler_params=on_vmem(),
        name="pack",
    )(at, *arrays, *prior_arrays)


def unpack_kernel(positions, in_ref, out_ref, loss_ref, tails, sems):
    seq_count, seg_count, _, width = in_ref.shape
    rows = out_ref.shape[0]
    spare = tails.shape[2]
    count = seg_count * seq_count
    tail = pltpu.make_async_copy(in_ref.at[:, :, rows : rows + spare, :], tails, sems.at[count])
    tail.start()
    copies = []
    for i in range(count):
        from_ref = in_ref.at[i // seg_count, i % seg_count, 0:rows, :]
        columns = slice(i * width, (i + 1) * width)
        copies.append(pltpu.make_async_copy(from_ref, out_ref.at[:, columns], sems.at[i]))
        copies[-1].start()
    tail.wait()
    parts = tails[...].reshape(-1, width).astype(jnp.float32)
    total = jnp.sum(jnp.sum(parts, axis=0, keepdims=True), axis=1, keepdims=True)
    loss_ref[...] = total / positions
    for copy in copies:
        copy.wait()


def unpack(blocks, rows, positions):
    seq_count, seg_count, _, width = blocks.shape
    spare = blocks.shape[2] - rows
    count = seg_count * seq_count
    return pl.pallas_call(
        functools.partial(unpack_kernel, positions),
        out_shape=(
            jax.ShapeDtypeStruct((rows, count * width), blocks.dtype),
            jax.ShapeDtypeStruct((1, 1), jnp.float32),
        ),
        in_specs=[pl.BlockSpec(memory_space=pl.ANY)],
        out_specs=(
            pl.BlockSpec(memory_space=pl.ANY),
            pl.BlockSpec(memory_space=pltpu.VMEM),
        ),
        scratch_shapes=[
            pltpu.VMEM((seq_count, seg_count, spare, width), blocks.dtype),
            pltpu.SemaphoreType.DMA((count + 1,)),
        ],
        compiler_params=on_vmem(8),
        name="unpack",
    )(blocks)


def matmul_t(a, b):
    return lax.dot_general(a, b, (((1,), (1,)), ((), ())), preferred_element_type=jnp.float32)


def t_matmul(a, b):
    return lax.dot_general(a, b, (((0,), (0,)), ((), ())), preferred_element_type=jnp.float32)


def matmul(a, b):
    return jnp.dot(a, b, preferred_element_type=jnp.float32)


def softmax_part(scores, rate):
    top = jnp.max(scores, axis=1, keepdims=True)
    return top, jnp.exp2((scores - top) * rate)


def merge_taps(fine, conv, comp, win, rows_f32):
    comp_rows, width = comp.shape
    rows_f32[...] = fine[:, 0:width].astype(jnp.float32)
    for r in range(RATE):
        taps = rows_f32[pl.ds(r, comp_rows, stride=RATE), :]
        win[:, r * width : (r + 1) * width] = taps.astype(jnp.bfloat16)
    comp[...] = matmul(win[...], conv[0]).astype(jnp.bfloat16)


def doc_bounds(starts_ref, g, seg_rows, comp_rows):
    def start_of(i):
        return jnp.where(i >= 0, starts_ref[jnp.maximum(i, 0)], seg_rows)

    b0, b1, b2 = start_of(g), start_of(g - 1), start_of(g - 2)
    s1 = jnp.where(b1 < seg_rows, b1, 0)
    s2 = jnp.where(b2 < seg_rows, b2, 0)
    memory_from = jnp.where((g >= 1) & (b1 >= seg_rows), s2, RATE * comp_rows)
    return b0, s1, memory_from


def memory_scores(scores, p0, b0, memory_from):
    place_q = p0 + lax.broadcasted_iota(jnp.int32, scores.shape, 0)
    place_k = RATE * lax.broadcasted_iota(jnp.int32, scores.shape, 1)
    return jnp.where((place_q < b0) & (place_k >= memory_from), scores, HIDDEN)


def own_scores(scores, p0, b0):
    place_q = p0 + lax.broadcasted_iota(jnp.int32, scores.shape, 0)
    place_k = lax.broadcasted_iota(jnp.int32, scores.shape, 1)
    seen = (place_k <= place_q) & ((place_k >= b0) | (place_q < b0))
    return jnp.where(seen, scores, HIDDEN)


def before_doc(step, p0, b0):
    return p0 + lax.broadcasted_iota(jnp.int32, (step, 1), 0) < b0


def head_kernel(
    dims, starts_ref, at_ref, recv_ref, prior_ref, conv_k_ref, conv_v_ref,
    out_ref, grad_ref, *rest,
):
    rows, seq_count, step = dims
    share_refs, rest = rest[: prior_ref.shape[1]], rest[prior_ref.shape[1] :]
    (
        out_rows, loss_rows, comp_ref, fine_k, fine_v, cat_k, cat_v, rows_f32,
        win_k, win_v, sums, losses, sems,
    ) = rest
    g = pl.program_id(0)
    seg_rows = rows * seq_count
    comp_rows = seg_rows // RATE
    _, seg_count, both_shares, width = prior_ref.shape
    share = both_shares // 2
    scale = 1.0 / math.sqrt(width)
    rate = math.log2(math.e) * scale
    bf16 = jnp.bfloat16

    @pl.when(g == 0)
    def _():
        cat_k[0:comp_rows, :] = jnp.zeros((comp_rows, width), bf16)
        cat_v[0:comp_rows, 0:width] = jnp.zeros((comp_rows, width), bf16)
        cat_v[:, width:] = jnp.ones((comp_rows + seg_rows, width), bf16)
        fine_v[:, width:] = jnp.ones((seg_rows, width), bf16)
        sums[...] = jnp.zeros_like(sums)
        losses[...] = jnp.zeros_like(losses)
        for s in range(seq_count):
            for i in range(seg_count):
                at = s * rows + i * share
                fine_k[at : at + share, :] = prior_ref[s, i, 0:share, :]
                fine_v[at : at + share, 0:width] = prior_ref[s, i, share:, :]

    @pl.when(g > 0)
    def _():
        fine_k[...] = cat_k[comp_rows:, :]
        fine_v[:, 0:width] = cat_v[comp_rows:, 0:width]

    cat_k[comp_rows:, :] = recv_ref[:, 0, rows : 2 * rows, :].reshape(seg_rows, width)
    cat_v[comp_rows:, 0:width] = recv_ref[:, 0, 2 * rows : 3 * rows, :].reshape(seg_rows, width)
    merge_taps(fine_k, conv_k_ref, comp_ref.at[0], win_k, rows_f32)
    merge_taps(fine_v, conv_v_ref, comp_ref.at[1], win_v, rows_f32)
    comp_k, comp_v = comp_ref[0], comp_ref[1]
    for i, share_ref in enumerate(share_refs):

        @pl.when(lax.rem(g - at_ref[0] + seg_count, seg_count) == i)
        def _():
            share_ref[...] = comp_ref[...]

    b0, s1, memory_from = doc_bounds(starts_ref, g, seg_rows, comp_rows)

    def queries(p0):
        return recv_ref[p0 // rows : (p0 + step) // rows, 0, 0:rows, :].reshape(step, width)

    def weighted(weights, values_and_ones):
        mix = matmul(weights.astype(bf16), values_and_ones)
        return mix[:, 0:width], mix[:, width:]

    def attend(fine_from_s1):
        fine, recon = {}, {}
        value_rows, key_rows = [], []

        def fine_scores(p0):
            return matmul_t(queries(p0), fine_k[...])

        def fine_part(p0, scores):
            top, weights = softmax_part(scores, rate)
            mix, total = weighted(weights, fine_v[...])
            recon[p0] = mix / total
            if fine_from_s1:
                place = lax.broadcasted_iota(jnp.int32, scores.shape, 1)
                top, weights = softmax_part(jnp.where(place >= s1, scores, HIDDEN), rate)
                mix, total = weighted(weights, fine_v[...])
            fine[p0] = top, mix, total

        def comp_scores(p0):
            return matmul_t(queries(p0), comp_k)

        def comp_part(p0, scores):
            _, comp_exp = softmax_part(scores, rate)
            total = jnp.sum(comp_exp, axis=1, keepdims=True)
            weights = comp_exp.astype(bf16)
            recon_comp = matmul(weights, comp_v) / total
            differ = recon.pop(p0) - recon_comp
            losses[...] += jnp.sum(differ * differ, axis=0, keepdims=True)
            out_grad = (-2.0 * differ / total).astype(bf16)
            inner = matmul_t(out_grad, comp_v)
            offset = jnp.sum(out_grad.astype(jnp.float32) * recon_comp, axis=1, keepdims=True)
            score_grad = (comp_exp * (inner - offset)).astype(bf16)
            value_rows.append(t_matmul(weights, out_grad))
            key_rows.append(t_matmul(score_grad, queries(p0)))

        def cat_scores(p0):
            scores = matmul_t(queries(p0), cat_k[0 : comp_rows + p0 + step, :])
            memory = memory_scores(scores[:, 0:comp_rows], p0, b0, memory_from)
            return jnp.concatenate((memory, own_scores(scores[:, comp_rows:], p0, b0)), axis=1)

        def cat_part(p0, scores):
            top, weights = softmax_part(scores, rate)
            mix, total = weighted(weights, cat_v[0 : comp_rows + p0 + step, :])
            fine_top, fine_mix, fine_total = fine.pop(p0)
            seen = before_doc(step, p0, b0)
            both = jnp.where(seen, jnp.maximum(top, fine_top), top)
            fine_share = jnp.where(seen, jnp.exp2((fine_top - both) * rate), 0.0)
            cat_share = jnp.exp2((top - both) * rate)
            mix = mix * cat_share + fine_mix * fine_share
            total = total * cat_share + fine_total * fine_share
            here = slice(p0 // rows, (p0 + step) // rows)
            out_rows[g, here] = (mix / total).astype(bf16).reshape(step // rows, rows, width)

        parts = [
            (p0, *part)
            for p0 in range(0, seg_rows, step)
            for part in ((fine_scores, fine_part), (cat_scores, cat_part), (comp_scores, comp_part))
        ]
        asked = [ask(p0) for p0, ask, _ in parts[:AHEAD]]
        for i, (p0, _, finish) in enumerate(parts):
            if i + AHEAD < len(parts):
                asked.append(parts[i + AHEAD][1](parts[i + AHEAD][0]))
            finish(p0, asked.pop(0))
        sums[0] += t_matmul(win_k[...], (sum(key_rows) * scale).astype(bf16))
        sums[1] += t_matmul(win_v[...], sum(value_rows).astype(bf16))

    @pl.when(s1 <= 0)
    def _():
        attend(False)

    @pl.when(s1 > 0)
    def _():
        attend(True)

    def copy_out(i):
        return pltpu.make_async_copy(out_rows.at[i], out_ref.at[:, i, 0:rows, :], sems.at[i])

    copy_out(g).start()
    cat_k[0:comp_rows, :] = comp_k
    cat_v[0:comp_rows, 0:width] = comp_v
    @pl.when(g == seg_count - 1)
    def _():
        left = losses[...]
        parts = []
        for _ in range(3):
            parts.append(left.astype(bf16).astype(jnp.float32))
            left = left - parts[-1]
        spare = loss_rows.shape[2]
        parts.append(jnp.zeros((spare - len(parts), width), jnp.float32))
        tail = jnp.concatenate(parts).astype(bf16)
        for s in range(seq_count):
            loss_rows[0, s] = tail
        copies = [
            pltpu.make_async_copy(
                loss_rows.at[0], out_ref.at[:, i, rows : rows + spare, :], sems.at[seg_count + i]
            )
            for i in range(seg_count)
        ]
        for copy in copies:
            copy.start()
        grad_ref[...] = sums[...].astype(bf16)
        for i in range(seg_count):
            copy_out(i).wait()
        for copy in copies:
            copy.wait()


def head(starts, at, recv, conv_keys, conv_values):
    seq_count, seg_count, block, width = recv.shape
    rows = block * seg_count // (3 * seg_count + 2)
    share = rows // seg_count
    seg_rows = rows * seq_count
    comp_rows = seg_rows // RATE
    step = math.gcd(seg_rows, STEP)
    bf16, f32 = jnp.bfloat16, jnp.float32
    shape = jax.ShapeDtypeStruct
    spare = 8
    comp_shape = (2, comp_rows, width)
    grad_shape = (2, RATE * width, width)
    conv = pl.BlockSpec((1, RATE * width, width), lambda g, starts, at: (at[0], 0, 0))

    def body(starts_ref, at_ref, *refs):
        head_kernel((rows, seq_count, step), starts_ref, at_ref, *refs)

    return pl.pallas_call(
        body,
        out_shape=(
            shape((seq_count, seg_count, rows + spare, width), bf16),
            shape(grad_shape, bf16),
            *[shape(comp_shape, bf16)] * seg_count,
        ),
        grid_spec=pltpu.PrefetchScalarGridSpec(
            num_scalar_prefetch=2,
            grid=(seg_count,),
            in_specs=[
                pl.BlockSpec((seq_count, 1, 3 * rows, width), lambda g, starts, at: (0, g, 0, 0)),
                pl.BlockSpec(
                    (seq_count, seg_count, 2 * share, width),
                    lambda g, starts, at: (0, 0, 3 * rows // (2 * share), 0),
                ),
                conv,
                conv,
            ],
            out_specs=(
                pl.BlockSpec(memory_space=pl.ANY),
                pl.BlockSpec(grad_shape, lambda g, starts, at: (0, 0, 0)),
                *[pl.BlockSpec(comp_shape, lambda g, starts, at: (0, 0, 0))] * seg_count,
            ),
            scratch_shapes=[
                pltpu.VMEM((seg_count, seq_count, rows, width), bf16),
                pltpu.VMEM((1, seq_count, spare, width), bf16),
                pltpu.VMEM((2, comp_rows, width), bf16),
                pltpu.VMEM((seg_rows, width), bf16),
                pltpu.VMEM((seg_rows, 2 * width), bf16),
                pltpu.VMEM((comp_rows + seg_rows, width), bf16),
                pltpu.VMEM((comp_rows + seg_rows, 2 * width), bf16),
                pltpu.VMEM((seg_rows, width), f32),
                pltpu.VMEM((comp_rows, RATE * width), bf16),
                pltpu.VMEM((comp_rows, RATE * width), bf16),
                pltpu.VMEM((2, RATE * width, width), f32),
                pltpu.VMEM((1, width), f32),
                pltpu.SemaphoreType.DMA((2 * seg_count,)),
            ],
        ),
        compiler_params=on_vmem(28),
        cost_estimate=pl.CostEstimate(
            flops=20 * seg_count * seg_rows * seg_rows * width, bytes_accessed=2**23, transcendentals=0
        ),
        name="head",
    )(starts, at, recv, recv, conv_keys, conv_values)


def share_kernel(at_ref, *refs):
    arrived, (comp_k_ref, comp_v_ref, grad_k_ref, grad_v_ref) = refs[:-4], refs[-4:]
    heads, _, width = grad_k_ref.shape
    for step, ref in enumerate(arrived[:heads]):
        head_at = lax.rem(at_ref[0] - step + heads, heads)
        columns = pl.ds(pl.multiple_of(head_at * width, width), width)
        comp_k_ref[:, columns] = ref[0]
        comp_v_ref[:, columns] = ref[1]
    for step, ref in enumerate(arrived[heads:]):
        grads = ref[...].astype(jnp.float32)
        grad_k_ref[at_ref[0] ^ step] = grads[0]
        grad_v_ref[at_ref[0] ^ step] = grads[1]


def shared(at, comps, grads):
    heads = len(comps)
    comp_rows, width = comps[0].shape[1:]
    arrived = [comps[0]]
    for step in range(1, heads):
        route = [(i, (i + step) % heads) for i in range(heads)]
        arrived.append(lax.ppermute(comps[step], "seg", route))
    held = {0: grads}
    bit = heads // 2
    while bit:
        route = [(i, i ^ bit) for i in range(heads)]
        came = [lax.ppermute(x, "seg", route) for x in held.values()]
        if bit > 1:
            came, arrived = lax.optimization_barrier((came, arrived))
        held |= {k ^ bit: x for k, x in zip(held, came)}
        bit //= 2
    arrived += [held[k] for k in range(heads)]
    comp = jax.ShapeDtypeStruct((comp_rows, heads * width), grads.dtype)
    grad = jax.ShapeDtypeStruct((heads, *grads.shape[1:]), jnp.float32)
    in_vmem = pl.BlockSpec(memory_space=pltpu.VMEM)
    return pl.pallas_call(
        share_kernel,
        out_shape=(comp, comp, grad, grad),
        in_specs=[pl.BlockSpec(memory_space=pltpu.SMEM), *[in_vmem] * len(arrived)],
        out_specs=(in_vmem,) * 4,
        compiler_params=on_vmem(12),
        name="shared",
    )(at, *arrived)


def head_on_device(
    queries, keys, values, prior_keys, prior_values, conv_keys, conv_values, doc_starts
):
    seq_count = lax.axis_size("seq")
    seg_count = lax.axis_size("seg")
    count = seg_count * seq_count
    rows = queries.shape[0]
    width = conv_keys.shape[2]
    at = lax.axis_index("seg").astype(jnp.int32).reshape(1)

    def exchanged(blocks):
        flat = blocks.reshape(count, -1, width)
        flat = lax.all_to_all(flat, BOTH, split_axis=0, concat_axis=0, tiled=True)
        return flat.reshape(blocks.shape)

    packed = pack(at, (queries, keys, values), (prior_keys, prior_values), seg_count, seq_count)
    attended, grads, *comps = head(doc_starts, at, exchanged(packed), conv_keys, conv_values)
    attended, loss = unpack(exchanged(attended), rows, count * rows)
    comp_keys, comp_values, grad_k, grad_v = shared(at, comps, grads)
    return (attended, comp_keys, comp_values, loss[0, 0], grad_k, grad_v)


def shifted_2(block, axis, distance):
    devices = range(lax.axis_size(axis))
    route = [(i - distance, i) for i in devices if i - distance in devices]
    return lax.ppermute(block, axis, route)


def pick_entry(small_table, wanted):
    return jnp.sum(jnp.where(jnp.arange(small_table.shape[0]) == wanted, small_table, 0))


def compress(source_rows, weight):
    head_count = weight.shape[0]
    head_width = weight.shape[2]
    windows = source_rows.reshape(source_rows.shape[0] // RATE, RATE, head_count, head_width)
    kernel = weight.reshape(head_count, RATE, head_width, head_width)
    merged = jnp.einsum("crhd,hrde->che", windows, kernel, preferred_element_type=jnp.float32)
    return merged.reshape(merged.shape[0], head_count * head_width).astype(jnp.bfloat16)


def on_device(queries, keys, values, prior_keys, prior_values, conv_keys, conv_values, doc_starts):
    seq_count = lax.axis_size("seq")
    seg_count = lax.axis_size("seg")
    group_index = lax.axis_index("seg")
    seg_rows = queries.shape[0] * seq_count
    head_count = conv_keys.shape[0]
    head_width = conv_keys.shape[2]
    comp_rows = seg_rows // RATE
    score_scale = 1.0 / math.sqrt(head_width)
    first_group = group_index == 0
    shifted = shifted_2(jnp.stack((keys, values)), "seg", 1)
    previous = jnp.where(first_group, jnp.stack((prior_keys, prior_values)), shifted)
    moved = (
        lax.all_to_all(queries, "seq", split_axis=1, concat_axis=0, tiled=True),
        lax.all_to_all(keys, "seq", split_axis=1, concat_axis=0, tiled=True),
        lax.all_to_all(values, "seq", split_axis=1, concat_axis=0, tiled=True),
        lax.all_to_all(previous[0], "seq", split_axis=1, concat_axis=0, tiled=True),
        lax.all_to_all(previous[1], "seq", split_axis=1, concat_axis=0, tiled=True),
    )
    query_heads = moved[0]
    key_heads = moved[1]
    value_heads = moved[2]
    fine_keys = moved[3]
    fine_values = moved[4]
    comp_keys = compress(fine_keys, conv_keys)
    comp_values = compress(fine_values, conv_values)
    memory = shifted_2(jnp.stack((comp_keys, comp_values)), "seg", 1)
    start_now = pick_entry(doc_starts, group_index)
    start_prev = jnp.where(group_index >= 1, pick_entry(doc_starts, group_index - 1), seg_rows)
    start_back = jnp.where(group_index >= 2, pick_entry(doc_starts, group_index - 2), seg_rows)
    lead_prev = jnp.where(start_prev < seg_rows, start_prev, 0)
    lead_back = jnp.where(start_back < seg_rows, start_back, 0)
    comp_open = (group_index >= 1) & (start_prev >= seg_rows)
    all_keys = jnp.concatenate((memory[0], fine_keys, key_heads), axis=0)
    all_values = jnp.concatenate((memory[1], fine_values, value_heads), axis=0)
    block_rows = math.gcd(seg_rows, 512)
    block_count = seg_rows // block_rows
    column = jnp.arange(comp_rows + 2 * seg_rows, dtype=jnp.int32)[None, :]
    comp_part = column < comp_rows
    fine_part = (column >= comp_rows) & (column < comp_rows + seg_rows)
    own_part = column >= comp_rows + seg_rows
    key_place = jnp.where(
        comp_part,
        RATE * column,
        jnp.where(fine_part, column - comp_rows, column - comp_rows - seg_rows),
    )

    def attend_block(flat_index):
        head_index = flat_index // block_count
        block_index = flat_index % block_count
        query_block = lax.dynamic_slice(
            query_heads,
            (block_index * block_rows, head_index * head_width),
            (block_rows, head_width),
        )
        key_block = lax.dynamic_slice_in_dim(all_keys, head_index * head_width, head_width, 1)
        value_block = lax.dynamic_slice_in_dim(all_values, head_index * head_width, head_width, 1)
        scores = (
            jnp.einsum("qd,kd->qk", query_block, key_block, preferred_element_type=jnp.float32)
            * score_scale
        )
        query_place = block_index * block_rows + jnp.arange(block_rows, dtype=jnp.int32)[:, None]
        before_doc = query_place < start_now
        seen_comp = comp_part & comp_open & before_doc & (key_place >= lead_back)
        seen_fine = fine_part & before_doc & (key_place >= lead_prev)
        seen_own = own_part & (key_place <= query_place) & ((key_place >= start_now) | before_doc)
        visible = seen_comp | seen_fine | seen_own
        row_top = jnp.max(jnp.where(visible, scores, -jnp.inf), axis=1, keepdims=True)
        weights = jnp.exp(jnp.where(visible, scores - row_top, -jnp.inf))
        row_total = jnp.sum(weights, axis=1, keepdims=True)
        mixed_rows = (
            jnp.dot(weights.astype(jnp.bfloat16), value_block, preferred_element_type=jnp.float32)
            / row_total
        )
        return mixed_rows.astype(jnp.bfloat16)

    pieces = lax.map(attend_block, jnp.arange(head_count * block_count, dtype=jnp.int32))
    attended_heads = (
        pieces.reshape(head_count, seg_rows, head_width)
        .transpose(1, 0, 2)
        .reshape(seg_rows, head_count * head_width)
    )
    attended = lax.all_to_all(attended_heads, "seq", split_axis=0, concat_axis=1, tiled=True)

    def recon_head(head_index):
        start_col = head_index * head_width
        query_full = lax.dynamic_slice_in_dim(query_heads, start_col, head_width, 1)
        fine_k = lax.dynamic_slice_in_dim(fine_keys, start_col, head_width, 1)
        fine_v = lax.dynamic_slice_in_dim(fine_values, start_col, head_width, 1)
        comp_k = lax.dynamic_slice_in_dim(comp_keys, start_col, head_width, 1)
        comp_v = lax.dynamic_slice_in_dim(comp_values, start_col, head_width, 1)

        def recon_step(running, block_index):
            loss_sum, value_acc, key_acc = running
            query_block = lax.dynamic_slice_in_dim(
                query_full, block_index * block_rows, block_rows, 0
            )
            fine_scores = (
                jnp.einsum("qd,kd->qk", query_block, fine_k, preferred_element_type=jnp.float32)
                * score_scale
            )
            fine_exp = jnp.exp(fine_scores - jnp.max(fine_scores, axis=1, keepdims=True))
            fine_total = jnp.sum(fine_exp, axis=1, keepdims=True)
            recon_fine = (
                jnp.dot(fine_exp.astype(jnp.bfloat16), fine_v, preferred_element_type=jnp.float32)
                / fine_total
            )
            comp_scores = (
                jnp.einsum("qd,kd->qk", query_block, comp_k, preferred_element_type=jnp.float32)
                * score_scale
            )
            comp_exp = jnp.exp(comp_scores - jnp.max(comp_scores, axis=1, keepdims=True))
            comp_total = jnp.sum(comp_exp, axis=1, keepdims=True)
            comp_weights = comp_exp.astype(jnp.bfloat16)
            recon_comp = (
                jnp.dot(comp_weights, comp_v, preferred_element_type=jnp.float32) / comp_total
            )
            differ = recon_fine - recon_comp
            out_grad = (-2.0 * differ / comp_total).astype(jnp.bfloat16)
            value_acc = value_acc + jnp.einsum(
                "qc,qd->cd", comp_weights, out_grad, preferred_element_type=jnp.float32
            )
            inner_grad = jnp.einsum(
                "qd,cd->qc", out_grad, comp_v, preferred_element_type=jnp.float32
            )
            row_offset = jnp.sum(out_grad.astype(jnp.float32) * recon_comp, axis=1, keepdims=True)
            score_grad = (comp_exp * (inner_grad - row_offset)).astype(jnp.bfloat16)
            key_acc = key_acc + jnp.einsum(
                "qc,qd->cd", score_grad, query_block, preferred_element_type=jnp.float32
            )
            return ((loss_sum + jnp.sum(differ * differ), value_acc, key_acc), None)

        zero_rows = jnp.zeros((comp_rows, head_width), jnp.float32)
        start_state = (jnp.zeros((), jnp.float32), zero_rows, zero_rows)
        (loss_sum, value_acc, key_acc), unused = lax.scan(
            recon_step, start_state, jnp.arange(block_count, dtype=jnp.int32)
        )
        key_grad = (key_acc * score_scale).astype(jnp.bfloat16)
        value_grad = value_acc.astype(jnp.bfloat16)
        windows_k = fine_k.reshape(comp_rows, RATE * head_width)
        windows_v = fine_v.reshape(comp_rows, RATE * head_width)
        grad_k = jnp.einsum("cw,cd->wd", windows_k, key_grad, preferred_element_type=jnp.float32)
        grad_v = jnp.einsum("cw,cd->wd", windows_v, value_grad, preferred_element_type=jnp.float32)
        return (loss_sum, grad_k, grad_v)

    losses, grad_k, grad_v = lax.map(recon_head, jnp.arange(head_count, dtype=jnp.int32))
    grad_k, grad_v = (
        lax.psum(grad_k.astype(jnp.bfloat16), "seg").astype(jnp.float32),
        lax.psum(grad_v.astype(jnp.bfloat16), "seg").astype(jnp.float32),
    )
    total_loss = lax.psum(jnp.sum(losses), ("seg", "seq"))
    recon_loss = total_loss / (seg_count * seg_rows)
    return (attended, comp_keys, comp_values, recon_loss, grad_k, grad_v)


def solution(mesh):
    def body(*arrays):
        heads, width = arrays[5].shape[0], arrays[5].shape[2]
        rows = arrays[0].shape[0]
        by_head = heads == mesh.shape["seg"] and width % 128 == 0
        by_head = by_head and all(n & (n - 1) == 0 for n in mesh.shape.values())
        by_head = by_head and heads % 2 == 0 and rows % (16 * heads) == 0 and 256 % rows == 0
        return (head_on_device if by_head else on_device)(*arrays)

    return jax.shard_map(
        body,
        mesh=mesh,
        in_specs=(
            P(("seg", "seq"), None),
            P(("seg", "seq"), None),
            P(("seg", "seq"), None),
            P("seq", None),
            P("seq", None),
            P("seq", None, None),
            P("seq", None, None),
            P(),
        ),
        out_specs=(
            P(("seg", "seq"), None),
            P("seg", "seq"),
            P("seg", "seq"),
            P(),
            P("seq", None, None),
            P("seq", None, None),
        ),
        check_vma=False,
    )
```

```python
import functools
import math

import jax
import jax.numpy as jnp
from jax import lax
from jax.experimental import pallas as pl
from jax.experimental.pallas import tpu as pltpu
from jax.sharding import PartitionSpec as P

RATE = 4
HIDDEN = -1e30
STEP = 512
AHEAD = 2
BOTH = ("seq", "seg")


def on_vmem(limit_mib=60):
    return pltpu.CompilerParams(vmem_limit_bytes=limit_mib * 2**20)


def pack_kernel(at_ref, *refs):
    del at_ref
    out_ref = refs[-1]
    seq_count, seg_count, _, width = out_ref.shape
    for s in range(seq_count):
        for r in range(seg_count):
            column = (s * seg_count + r) * width
            row = 0
            for ref in refs[:-1]:
                rows = ref.shape[0]
                out_ref[s, r, row : row + rows, :] = ref[:, column : column + width]
                row += rows


def pack(at, arrays, prior_arrays, seg_count, seq_count):
    rows, columns = arrays[0].shape
    width = columns // (seg_count * seq_count)
    share = rows // seg_count
    block = len(arrays) * rows + len(prior_arrays) * share
    steps = 2
    wide = columns // steps
    return pl.pallas_call(
        pack_kernel,
        out_shape=jax.ShapeDtypeStruct((seq_count, seg_count, block, width), arrays[0].dtype),
        grid_spec=pltpu.PrefetchScalarGridSpec(
            num_scalar_prefetch=1,
            grid=(steps,),
            in_specs=[
                *[pl.BlockSpec((rows, wide), lambda s, at: (0, s))] * len(arrays),
                *[pl.BlockSpec((share, wide), lambda s, at: (at[0], s))] * len(prior_arrays),
            ],
            out_specs=pl.BlockSpec(
                (seq_count // steps, seg_count, block, width), lambda s, at: (s, 0, 0, 0)
            ),
        ),
        compiler_params=on_vmem(),
        name="pack",
    )(at, *arrays, *prior_arrays)


def unpack_kernel(positions, in_ref, out_ref, loss_ref, tails, sems):
    seq_count, seg_count, _, width = in_ref.shape
    rows = out_ref.shape[0]
    spare = tails.shape[2]
    count = seg_count * seq_count
    tail = pltpu.make_async_copy(in_ref.at[:, :, rows : rows + spare, :], tails, sems.at[count])
    tail.start()
    copies = []
    for i in range(count):
        from_ref = in_ref.at[i // seg_count, i % seg_count, 0:rows, :]
        columns = slice(i * width, (i + 1) * width)
        copies.append(pltpu.make_async_copy(from_ref, out_ref.at[:, columns], sems.at[i]))
        copies[-1].start()
    tail.wait()
    parts = tails[...].reshape(-1, width).astype(jnp.float32)
    total = jnp.sum(jnp.sum(parts, axis=0, keepdims=True), axis=1, keepdims=True)
    loss_ref[...] = total / positions
    for copy in copies:
        copy.wait()


def unpack(blocks, rows, positions):
    seq_count, seg_count, _, width = blocks.shape
    spare = blocks.shape[2] - rows
    count = seg_count * seq_count
    return pl.pallas_call(
        functools.partial(unpack_kernel, positions),
        out_shape=(
            jax.ShapeDtypeStruct((rows, count * width), blocks.dtype),
            jax.ShapeDtypeStruct((1, 1), jnp.float32),
        ),
        in_specs=[pl.BlockSpec(memory_space=pl.ANY)],
        out_specs=(
            pl.BlockSpec(memory_space=pl.ANY),
            pl.BlockSpec(memory_space=pltpu.VMEM),
        ),
        scratch_shapes=[
            pltpu.VMEM((seq_count, seg_count, spare, width), blocks.dtype),
            pltpu.SemaphoreType.DMA((count + 1,)),
        ],
        compiler_params=on_vmem(8),
        name="unpack",
    )(blocks)


def matmul_t(a, b):
    return lax.dot_general(a, b, (((1,), (1,)), ((), ())), preferred_element_type=jnp.float32)


def t_matmul(a, b):
    return lax.dot_general(a, b, (((0,), (0,)), ((), ())), preferred_element_type=jnp.float32)


def matmul(a, b):
    return jnp.dot(a, b, preferred_element_type=jnp.float32)


def softmax_part(scores, rate):
    top = jnp.max(scores, axis=1, keepdims=True)
    return top, jnp.exp2((scores - top) * rate)


def merge_taps(fine, conv, comp, win, rows_f32):
    comp_rows, width = comp.shape
    rows_f32[...] = fine[:, 0:width].astype(jnp.float32)
    for r in range(RATE):
        taps = rows_f32[pl.ds(r, comp_rows, stride=RATE), :]
        win[:, r * width : (r + 1) * width] = taps.astype(jnp.bfloat16)
    comp[...] = matmul(win[...], conv[0]).astype(jnp.bfloat16)


def doc_bounds(starts_ref, g, seg_rows, comp_rows):
    def start_of(i):
        return jnp.where(i >= 0, starts_ref[jnp.maximum(i, 0)], seg_rows)

    b0, b1, b2 = start_of(g), start_of(g - 1), start_of(g - 2)
    s1 = jnp.where(b1 < seg_rows, b1, 0)
    s2 = jnp.where(b2 < seg_rows, b2, 0)
    memory_from = jnp.where((g >= 1) & (b1 >= seg_rows), s2, RATE * comp_rows)
    return b0, s1, memory_from


def memory_scores(scores, p0, b0, memory_from):
    place_q = p0 + lax.broadcasted_iota(jnp.int32, scores.shape, 0)
    place_k = RATE * lax.broadcasted_iota(jnp.int32, scores.shape, 1)
    return jnp.where((place_q < b0) & (place_k >= memory_from), scores, HIDDEN)


def own_scores(scores, p0, b0):
    place_q = p0 + lax.broadcasted_iota(jnp.int32, scores.shape, 0)
    place_k = lax.broadcasted_iota(jnp.int32, scores.shape, 1)
    seen = (place_k <= place_q) & ((place_k >= b0) | (place_q < b0))
    return jnp.where(seen, scores, HIDDEN)


def before_doc(step, p0, b0):
    return p0 + lax.broadcasted_iota(jnp.int32, (step, 1), 0) < b0


def head_kernel(
    dims, starts_ref, at_ref, recv_ref, prior_ref, conv_k_ref, conv_v_ref,
    out_ref, grad_ref, *rest,
):
    rows, seq_count, step = dims
    share_refs, rest = rest[: prior_ref.shape[1]], rest[prior_ref.shape[1] :]
    (
        out_rows, loss_rows, comp_ref, fine_k, fine_v, cat_k, cat_v, rows_f32,
        win_k, win_v, sums, losses, sems,
    ) = rest
    g = pl.program_id(0)
    seg_rows = rows * seq_count
    comp_rows = seg_rows // RATE
    _, seg_count, both_shares, width = prior_ref.shape
    share = both_shares // 2
    scale = 1.0 / math.sqrt(width)
    rate = math.log2(math.e) * scale
    bf16 = jnp.bfloat16

    @pl.when(g == 0)
    def _():
        cat_k[0:comp_rows, :] = jnp.zeros((comp_rows, width), bf16)
        cat_v[0:comp_rows, 0:width] = jnp.zeros((comp_rows, width), bf16)
        cat_v[:, width:] = jnp.ones((comp_rows + seg_rows, width), bf16)
        fine_v[:, width:] = jnp.ones((seg_rows, width), bf16)
        sums[...] = jnp.zeros_like(sums)
        losses[...] = jnp.zeros_like(losses)
        for s in range(seq_count):
            for i in range(seg_count):
                at = s * rows + i * share
                fine_k[at : at + share, :] = prior_ref[s, i, 0:share, :]
                fine_v[at : at + share, 0:width] = prior_ref[s, i, share:, :]

    @pl.when(g > 0)
    def _():
        fine_k[...] = cat_k[comp_rows:, :]
        fine_v[:, 0:width] = cat_v[comp_rows:, 0:width]

    cat_k[comp_rows:, :] = recv_ref[:, 0, rows : 2 * rows, :].reshape(seg_rows, width)
    cat_v[comp_rows:, 0:width] = recv_ref[:, 0, 2 * rows : 3 * rows, :].reshape(seg_rows, width)
    merge_taps(fine_k, conv_k_ref, comp_ref.at[0], win_k, rows_f32)
    merge_taps(fine_v, conv_v_ref, comp_ref.at[1], win_v, rows_f32)
    comp_k, comp_v = comp_ref[0], comp_ref[1]
    for i, share_ref in enumerate(share_refs):

        @pl.when(lax.rem(g - at_ref[0] + seg_count, seg_count) == i)
        def _():
            share_ref[...] = comp_ref[...]

    b0, s1, memory_from = doc_bounds(starts_ref, g, seg_rows, comp_rows)

    def queries(p0, size=step):
        return recv_ref[p0 // rows : (p0 + size) // rows, 0, 0:rows, :].reshape(size, width)

    half = max(step // 2, rows)

    def weighted(weights, values_and_ones):
        mix = matmul(weights.astype(bf16), values_and_ones)
        return mix[:, 0:width], mix[:, width:]

    def attend(fine_from_s1):
        fine, recon = {}, {}
        value_rows, key_rows = [], []

        def fine_scores(p0):
            return matmul_t(queries(p0), fine_k[...])

        def fine_part(p0, scores):
            top, weights = softmax_part(scores, rate)
            mix, total = weighted(weights, fine_v[...])
            recon[p0] = mix / total
            if fine_from_s1:
                place = lax.broadcasted_iota(jnp.int32, scores.shape, 1)
                top, weights = softmax_part(jnp.where(place >= s1, scores, HIDDEN), rate)
                mix, total = weighted(weights, fine_v[...])
            fine[p0] = top, mix, total

        def comp_scores(p0):
            return matmul_t(queries(p0), comp_k)

        def comp_part(p0, scores):
            _, comp_exp = softmax_part(scores, rate)
            total = jnp.sum(comp_exp, axis=1, keepdims=True)
            weights = comp_exp.astype(bf16)
            recon_comp = matmul(weights, comp_v) / total
            differ = recon.pop(p0) - recon_comp
            losses[...] += jnp.sum(differ * differ, axis=0, keepdims=True)
            out_grad = (-2.0 * differ / total).astype(bf16)
            inner = matmul_t(out_grad, comp_v)
            offset = jnp.sum(out_grad.astype(jnp.float32) * recon_comp, axis=1, keepdims=True)
            score_grad = (comp_exp * (inner - offset)).astype(bf16)
            value_rows.append(t_matmul(weights, out_grad))
            key_rows.append(t_matmul(score_grad, queries(p0)))

        def cat_scores(p0):
            scores = matmul_t(queries(p0, half), cat_k[0 : comp_rows + p0 + half, :])
            memory = memory_scores(scores[:, 0:comp_rows], p0, b0, memory_from)
            return jnp.concatenate((memory, own_scores(scores[:, comp_rows:], p0, b0)), axis=1)

        def cat_part(p0, scores):
            top, weights = softmax_part(scores, rate)
            mix, total = weighted(weights, cat_v[0 : comp_rows + p0 + half, :])
            at = p0 % step
            fine_top, fine_mix, fine_total = (x[at : at + half] for x in fine[p0 - at])
            seen = before_doc(half, p0, b0)
            both = jnp.where(seen, jnp.maximum(top, fine_top), top)
            fine_share = jnp.where(seen, jnp.exp2((fine_top - both) * rate), 0.0)
            cat_share = jnp.exp2((top - both) * rate)
            mix = mix * cat_share + fine_mix * fine_share
            total = total * cat_share + fine_total * fine_share
            here = slice(p0 // rows, (p0 + half) // rows)
            out_rows[g, here] = (mix / total).astype(bf16).reshape(half // rows, rows, width)

        parts = [
            part
            for p0 in range(0, seg_rows, step)
            for part in (
                (p0, fine_scores, fine_part),
                *[(p, cat_scores, cat_part) for p in range(p0, p0 + step, half)],
                (p0, comp_scores, comp_part),
            )
        ]
        asked = [ask(p0) for p0, ask, _ in parts[:AHEAD]]
        for i, (p0, _, finish) in enumerate(parts):
            if i + AHEAD < len(parts):
                asked.append(parts[i + AHEAD][1](parts[i + AHEAD][0]))
            finish(p0, asked.pop(0))
        sums[0] += t_matmul(win_k[...], (sum(key_rows) * scale).astype(bf16))
        sums[1] += t_matmul(win_v[...], sum(value_rows).astype(bf16))

    @pl.when(s1 <= 0)
    def _():
        attend(False)

    @pl.when(s1 > 0)
    def _():
        attend(True)

    def copy_out(i):
        return pltpu.make_async_copy(out_rows.at[i], out_ref.at[:, i, 0:rows, :], sems.at[i])

    copy_out(g).start()
    cat_k[0:comp_rows, :] = comp_k
    cat_v[0:comp_rows, 0:width] = comp_v
    @pl.when(g == seg_count - 1)
    def _():
        left = losses[...]
        parts = []
        for _ in range(3):
            parts.append(left.astype(bf16).astype(jnp.float32))
            left = left - parts[-1]
        spare = loss_rows.shape[2]
        parts.append(jnp.zeros((spare - len(parts), width), jnp.float32))
        tail = jnp.concatenate(parts).astype(bf16)
        for s in range(seq_count):
            loss_rows[0, s] = tail
        copies = [
            pltpu.make_async_copy(
                loss_rows.at[0], out_ref.at[:, i, rows : rows + spare, :], sems.at[seg_count + i]
            )
            for i in range(seg_count)
        ]
        for copy in copies:
            copy.start()
        grad_ref[...] = sums[...].astype(bf16)
        for i in range(seg_count):
            copy_out(i).wait()
        for copy in copies:
            copy.wait()


def head(starts, at, recv, conv_keys, conv_values):
    seq_count, seg_count, block, width = recv.shape
    rows = block * seg_count // (3 * seg_count + 2)
    share = rows // seg_count
    seg_rows = rows * seq_count
    comp_rows = seg_rows // RATE
    step = math.gcd(seg_rows, STEP)
    bf16, f32 = jnp.bfloat16, jnp.float32
    shape = jax.ShapeDtypeStruct
    spare = 8
    comp_shape = (2, comp_rows, width)
    grad_shape = (2, RATE * width, width)
    conv = pl.BlockSpec((1, RATE * width, width), lambda g, starts, at: (at[0], 0, 0))

    def body(starts_ref, at_ref, *refs):
        head_kernel((rows, seq_count, step), starts_ref, at_ref, *refs)

    return pl.pallas_call(
        body,
        out_shape=(
            shape((seq_count, seg_count, rows + spare, width), bf16),
            shape(grad_shape, bf16),
            *[shape(comp_shape, bf16)] * seg_count,
        ),
        grid_spec=pltpu.PrefetchScalarGridSpec(
            num_scalar_prefetch=2,
            grid=(seg_count,),
            in_specs=[
                pl.BlockSpec((seq_count, 1, 3 * rows, width), lambda g, starts, at: (0, g, 0, 0)),
                pl.BlockSpec(
                    (seq_count, seg_count, 2 * share, width),
                    lambda g, starts, at: (0, 0, 3 * rows // (2 * share), 0),
                ),
                conv,
                conv,
            ],
            out_specs=(
                pl.BlockSpec(memory_space=pl.ANY),
                pl.BlockSpec(grad_shape, lambda g, starts, at: (0, 0, 0)),
                *[pl.BlockSpec(comp_shape, lambda g, starts, at: (0, 0, 0))] * seg_count,
            ),
            scratch_shapes=[
                pltpu.VMEM((seg_count, seq_count, rows, width), bf16),
                pltpu.VMEM((1, seq_count, spare, width), bf16),
                pltpu.VMEM((2, comp_rows, width), bf16),
                pltpu.VMEM((seg_rows, width), bf16),
                pltpu.VMEM((seg_rows, 2 * width), bf16),
                pltpu.VMEM((comp_rows + seg_rows, width), bf16),
                pltpu.VMEM((comp_rows + seg_rows, 2 * width), bf16),
                pltpu.VMEM((seg_rows, width), f32),
                pltpu.VMEM((comp_rows, RATE * width), bf16),
                pltpu.VMEM((comp_rows, RATE * width), bf16),
                pltpu.VMEM((2, RATE * width, width), f32),
                pltpu.VMEM((1, width), f32),
                pltpu.SemaphoreType.DMA((2 * seg_count,)),
            ],
        ),
        compiler_params=on_vmem(28),
        cost_estimate=pl.CostEstimate(
            flops=20 * seg_count * seg_rows * seg_rows * width, bytes_accessed=2**23, transcendentals=0
        ),
        name="head",
    )(starts, at, recv, recv, conv_keys, conv_values)


def share_kernel(at_ref, *refs):
    arrived, (comp_k_ref, comp_v_ref, grad_k_ref, grad_v_ref) = refs[:-4], refs[-4:]
    heads, _, width = grad_k_ref.shape
    for step, ref in enumerate(arrived[:heads]):
        head_at = lax.rem(at_ref[0] - step + heads, heads)
        columns = pl.ds(pl.multiple_of(head_at * width, width), width)
        comp_k_ref[:, columns] = ref[0]
        comp_v_ref[:, columns] = ref[1]
    for step, ref in enumerate(arrived[heads:]):
        grads = ref[...].astype(jnp.float32)
        grad_k_ref[at_ref[0] ^ step] = grads[0]
        grad_v_ref[at_ref[0] ^ step] = grads[1]


def shared(at, comps, grads):
    heads = len(comps)
    comp_rows, width = comps[0].shape[1:]
    arrived = [comps[0]]
    for step in range(1, heads):
        route = [(i, (i + step) % heads) for i in range(heads)]
        arrived.append(lax.ppermute(comps[step], "seg", route))
    held = {0: grads}
    bit = heads // 2
    while bit:
        route = [(i, i ^ bit) for i in range(heads)]
        came = [lax.ppermute(x, "seg", route) for x in held.values()]
        if bit > 1:
            came, arrived = lax.optimization_barrier((came, arrived))
        held |= {k ^ bit: x for k, x in zip(held, came)}
        bit //= 2
    arrived += [held[k] for k in range(heads)]
    comp = jax.ShapeDtypeStruct((comp_rows, heads * width), grads.dtype)
    grad = jax.ShapeDtypeStruct((heads, *grads.shape[1:]), jnp.float32)
    in_vmem = pl.BlockSpec(memory_space=pltpu.VMEM)
    return pl.pallas_call(
        share_kernel,
        out_shape=(comp, comp, grad, grad),
        in_specs=[pl.BlockSpec(memory_space=pltpu.SMEM), *[in_vmem] * len(arrived)],
        out_specs=(in_vmem,) * 4,
        compiler_params=on_vmem(12),
        name="shared",
    )(at, *arrived)


def head_on_device(
    queries, keys, values, prior_keys, prior_values, conv_keys, conv_values, doc_starts
):
    seq_count = lax.axis_size("seq")
    seg_count = lax.axis_size("seg")
    count = seg_count * seq_count
    rows = queries.shape[0]
    width = conv_keys.shape[2]
    at = lax.axis_index("seg").astype(jnp.int32).reshape(1)

    def exchanged(blocks):
        flat = blocks.reshape(count, -1, width)
        flat = lax.all_to_all(flat, BOTH, split_axis=0, concat_axis=0, tiled=True)
        return flat.reshape(blocks.shape)

    packed = pack(at, (queries, keys, values), (prior_keys, prior_values), seg_count, seq_count)
    attended, grads, *comps = head(doc_starts, at, exchanged(packed), conv_keys, conv_values)
    attended, loss = unpack(exchanged(attended), rows, count * rows)
    comp_keys, comp_values, grad_k, grad_v = shared(at, comps, grads)
    return (attended, comp_keys, comp_values, loss[0, 0], grad_k, grad_v)


def shifted_2(block, axis, distance):
    devices = range(lax.axis_size(axis))
    route = [(i - distance, i) for i in devices if i - distance in devices]
    return lax.ppermute(block, axis, route)


def pick_entry(small_table, wanted):
    return jnp.sum(jnp.where(jnp.arange(small_table.shape[0]) == wanted, small_table, 0))


def compress(source_rows, weight):
    head_count = weight.shape[0]
    head_width = weight.shape[2]
    windows = source_rows.reshape(source_rows.shape[0] // RATE, RATE, head_count, head_width)
    kernel = weight.reshape(head_count, RATE, head_width, head_width)
    merged = jnp.einsum("crhd,hrde->che", windows, kernel, preferred_element_type=jnp.float32)
    return merged.reshape(merged.shape[0], head_count * head_width).astype(jnp.bfloat16)


def on_device(queries, keys, values, prior_keys, prior_values, conv_keys, conv_values, doc_starts):
    seq_count = lax.axis_size("seq")
    seg_count = lax.axis_size("seg")
    group_index = lax.axis_index("seg")
    seg_rows = queries.shape[0] * seq_count
    head_count = conv_keys.shape[0]
    head_width = conv_keys.shape[2]
    comp_rows = seg_rows // RATE
    score_scale = 1.0 / math.sqrt(head_width)
    first_group = group_index == 0
    shifted = shifted_2(jnp.stack((keys, values)), "seg", 1)
    previous = jnp.where(first_group, jnp.stack((prior_keys, prior_values)), shifted)
    moved = (
        lax.all_to_all(queries, "seq", split_axis=1, concat_axis=0, tiled=True),
        lax.all_to_all(keys, "seq", split_axis=1, concat_axis=0, tiled=True),
        lax.all_to_all(values, "seq", split_axis=1, concat_axis=0, tiled=True),
        lax.all_to_all(previous[0], "seq", split_axis=1, concat_axis=0, tiled=True),
        lax.all_to_all(previous[1], "seq", split_axis=1, concat_axis=0, tiled=True),
    )
    query_heads = moved[0]
    key_heads = moved[1]
    value_heads = moved[2]
    fine_keys = moved[3]
    fine_values = moved[4]
    comp_keys = compress(fine_keys, conv_keys)
    comp_values = compress(fine_values, conv_values)
    memory = shifted_2(jnp.stack((comp_keys, comp_values)), "seg", 1)
    start_now = pick_entry(doc_starts, group_index)
    start_prev = jnp.where(group_index >= 1, pick_entry(doc_starts, group_index - 1), seg_rows)
    start_back = jnp.where(group_index >= 2, pick_entry(doc_starts, group_index - 2), seg_rows)
    lead_prev = jnp.where(start_prev < seg_rows, start_prev, 0)
    lead_back = jnp.where(start_back < seg_rows, start_back, 0)
    comp_open = (group_index >= 1) & (start_prev >= seg_rows)
    all_keys = jnp.concatenate((memory[0], fine_keys, key_heads), axis=0)
    all_values = jnp.concatenate((memory[1], fine_values, value_heads), axis=0)
    block_rows = math.gcd(seg_rows, 512)
    block_count = seg_rows // block_rows
    column = jnp.arange(comp_rows + 2 * seg_rows, dtype=jnp.int32)[None, :]
    comp_part = column < comp_rows
    fine_part = (column >= comp_rows) & (column < comp_rows + seg_rows)
    own_part = column >= comp_rows + seg_rows
    key_place = jnp.where(
        comp_part,
        RATE * column,
        jnp.where(fine_part, column - comp_rows, column - comp_rows - seg_rows),
    )

    def attend_block(flat_index):
        head_index = flat_index // block_count
        block_index = flat_index % block_count
        query_block = lax.dynamic_slice(
            query_heads,
            (block_index * block_rows, head_index * head_width),
            (block_rows, head_width),
        )
        key_block = lax.dynamic_slice_in_dim(all_keys, head_index * head_width, head_width, 1)
        value_block = lax.dynamic_slice_in_dim(all_values, head_index * head_width, head_width, 1)
        scores = (
            jnp.einsum("qd,kd->qk", query_block, key_block, preferred_element_type=jnp.float32)
            * score_scale
        )
        query_place = block_index * block_rows + jnp.arange(block_rows, dtype=jnp.int32)[:, None]
        before_doc = query_place < start_now
        seen_comp = comp_part & comp_open & before_doc & (key_place >= lead_back)
        seen_fine = fine_part & before_doc & (key_place >= lead_prev)
        seen_own = own_part & (key_place <= query_place) & ((key_place >= start_now) | before_doc)
        visible = seen_comp | seen_fine | seen_own
        row_top = jnp.max(jnp.where(visible, scores, -jnp.inf), axis=1, keepdims=True)
        weights = jnp.exp(jnp.where(visible, scores - row_top, -jnp.inf))
        row_total = jnp.sum(weights, axis=1, keepdims=True)
        mixed_rows = (
            jnp.dot(weights.astype(jnp.bfloat16), value_block, preferred_element_type=jnp.float32)
            / row_total
        )
        return mixed_rows.astype(jnp.bfloat16)

    pieces = lax.map(attend_block, jnp.arange(head_count * block_count, dtype=jnp.int32))
    attended_heads = (
        pieces.reshape(head_count, seg_rows, head_width)
        .transpose(1, 0, 2)
        .reshape(seg_rows, head_count * head_width)
    )
    attended = lax.all_to_all(attended_heads, "seq", split_axis=0, concat_axis=1, tiled=True)

    def recon_head(head_index):
        start_col = head_index * head_width
        query_full = lax.dynamic_slice_in_dim(query_heads, start_col, head_width, 1)
        fine_k = lax.dynamic_slice_in_dim(fine_keys, start_col, head_width, 1)
        fine_v = lax.dynamic_slice_in_dim(fine_values, start_col, head_width, 1)
        comp_k = lax.dynamic_slice_in_dim(comp_keys, start_col, head_width, 1)
        comp_v = lax.dynamic_slice_in_dim(comp_values, start_col, head_width, 1)

        def recon_step(running, block_index):
            loss_sum, value_acc, key_acc = running
            query_block = lax.dynamic_slice_in_dim(
                query_full, block_index * block_rows, block_rows, 0
            )
            fine_scores = (
                jnp.einsum("qd,kd->qk", query_block, fine_k, preferred_element_type=jnp.float32)
                * score_scale
            )
            fine_exp = jnp.exp(fine_scores - jnp.max(fine_scores, axis=1, keepdims=True))
            fine_total = jnp.sum(fine_exp, axis=1, keepdims=True)
            recon_fine = (
                jnp.dot(fine_exp.astype(jnp.bfloat16), fine_v, preferred_element_type=jnp.float32)
                / fine_total
            )
            comp_scores = (
                jnp.einsum("qd,kd->qk", query_block, comp_k, preferred_element_type=jnp.float32)
                * score_scale
            )
            comp_exp = jnp.exp(comp_scores - jnp.max(comp_scores, axis=1, keepdims=True))
            comp_total = jnp.sum(comp_exp, axis=1, keepdims=True)
            comp_weights = comp_exp.astype(jnp.bfloat16)
            recon_comp = (
                jnp.dot(comp_weights, comp_v, preferred_element_type=jnp.float32) / comp_total
            )
            differ = recon_fine - recon_comp
            out_grad = (-2.0 * differ / comp_total).astype(jnp.bfloat16)
            value_acc = value_acc + jnp.einsum(
                "qc,qd->cd", comp_weights, out_grad, preferred_element_type=jnp.float32
            )
            inner_grad = jnp.einsum(
                "qd,cd->qc", out_grad, comp_v, preferred_element_type=jnp.float32
            )
            row_offset = jnp.sum(out_grad.astype(jnp.float32) * recon_comp, axis=1, keepdims=True)
            score_grad = (comp_exp * (inner_grad - row_offset)).astype(jnp.bfloat16)
            key_acc = key_acc + jnp.einsum(
                "qc,qd->cd", score_grad, query_block, preferred_element_type=jnp.float32
            )
            return ((loss_sum + jnp.sum(differ * differ), value_acc, key_acc), None)

        zero_rows = jnp.zeros((comp_rows, head_width), jnp.float32)
        start_state = (jnp.zeros((), jnp.float32), zero_rows, zero_rows)
        (loss_sum, value_acc, key_acc), unused = lax.scan(
            recon_step, start_state, jnp.arange(block_count, dtype=jnp.int32)
        )
        key_grad = (key_acc * score_scale).astype(jnp.bfloat16)
        value_grad = value_acc.astype(jnp.bfloat16)
        windows_k = fine_k.reshape(comp_rows, RATE * head_width)
        windows_v = fine_v.reshape(comp_rows, RATE * head_width)
        grad_k = jnp.einsum("cw,cd->wd", windows_k, key_grad, preferred_element_type=jnp.float32)
        grad_v = jnp.einsum("cw,cd->wd", windows_v, value_grad, preferred_element_type=jnp.float32)
        return (loss_sum, grad_k, grad_v)

    losses, grad_k, grad_v = lax.map(recon_head, jnp.arange(head_count, dtype=jnp.int32))
    grad_k, grad_v = (
        lax.psum(grad_k.astype(jnp.bfloat16), "seg").astype(jnp.float32),
        lax.psum(grad_v.astype(jnp.bfloat16), "seg").astype(jnp.float32),
    )
    total_loss = lax.psum(jnp.sum(losses), ("seg", "seq"))
    recon_loss = total_loss / (seg_count * seg_rows)
    return (attended, comp_keys, comp_values, recon_loss, grad_k, grad_v)


def solution(mesh):
    def body(*arrays):
        heads, width = arrays[5].shape[0], arrays[5].shape[2]
        rows = arrays[0].shape[0]
        by_head = heads == mesh.shape["seg"] and width % 128 == 0
        by_head = by_head and all(n & (n - 1) == 0 for n in mesh.shape.values())
        by_head = by_head and heads % 2 == 0 and rows % (16 * heads) == 0 and 256 % rows == 0
        return (head_on_device if by_head else on_device)(*arrays)

    return jax.shard_map(
        body,
        mesh=mesh,
        in_specs=(
            P(("seg", "seq"), None),
            P(("seg", "seq"), None),
            P(("seg", "seq"), None),
            P("seq", None),
            P("seq", None),
            P("seq", None, None),
            P("seq", None, None),
            P(),
        ),
        out_specs=(
            P(("seg", "seq"), None),
            P("seg", "seq"),
            P("seg", "seq"),
            P(),
            P("seq", None, None),
            P("seq", None, None),
        ),
        check_vma=False,
    )
```
